32 devices in a mesh: grp: 4 (over x, core), rep: 8 (over z, y).
Axes of the slice: x: 2, y: 2, z: 4, core: 2. Of those that a mesh axis runs over, the one named last changes fastest.
Arguments:
- features: bfloat16 [16384, 768], P(('grp', 'rep')), may hold values from -6 to 6
- fetch_row: int32 [16, 512], P('grp', 'rep'), may hold values from 0 to 511
- live_count: int32 [16, 8], P('grp', 'rep'), may hold values from 16 to 64, as said below
- seed_features: bfloat16 [16384, 768], P(('grp', 'rep')), may hold values from -6 to 6
- tile_block: int32 [128, 2], P(('grp', 'rep')), may hold values from 0 to 1, each once within a row
- tile_weight: bfloat16 [128, 2, 128, 128], P(('grp', 'rep')), may hold values from -0.375 to 0.375
- self_weight: bfloat16 [768, 512], replicated, may hold values from -0.21875 to 0.21875
- neighbour_weight: bfloat16 [768, 512], replicated, may hold values from -0.21875 to 0.21875
- layer_bias: float32 [512], replicated, may hold values from -4 to 4
- cotangent: bfloat16 [16384, 512], P(('grp', 'rep')), may hold values from -6 to 6
Outputs:
- weight_grad: float32 [512, 768], P('grp', 'rep')
The draws below stay inside these ranges and needn't reach their ends.
Inputs may be any that keep to these rules, and one draw needn't show every extreme that they name: `live_count`: slots at or past the count are padding. In every draw, for each rep index some owner is asked for all 64 slots by every device of its group. `tile_block`: each row names every block of a device's fetched rows once.
All inputs are finite; a program needn't handle non-finite values.
Results may differ from the reference program's by a relative error of at most 0.0043.
Values may be sent and summed in bfloat16 or wider, within the bound.
A program may use at most 64 MiB of HBM per device.

```python
import jax
import jax.numpy as jnp
from jax import lax

FEAT = 768
HID = 512
TGT = 512
SLOTS = 64
ROWS_DEV = 512
FETCH = 256
SEEDS = 16384
N_GRP = 4
N_REP = 8


def draw_live_count(key, part):
    key = jax.random.fold_in(key, 11)
    key_base, key_hot = jax.random.split(key)
    base_count = jax.random.randint(key_base, (N_GRP * N_GRP, N_REP), SLOTS // 4, SLOTS + 1)
    hot_owner = jax.random.randint(key_hot, (1, N_REP), 0, N_GRP)
    peer_ix = (jnp.arange(N_GRP * N_GRP, dtype=jnp.int32) % N_GRP)[:, None]
    return jnp.where(peer_ix == hot_owner, SLOTS, base_count).astype(jnp.int32)


def place_ends(values, key, least, largest):
    longest = values.shape.index(max(values.shape))
    spots = []
    for shift in (0, 1):
        where = [jax.random.randint(jax.random.fold_in(key, axis), (), 0, length) for axis, length in enumerate(values.shape)]
        where[longest] = (where[longest] + shift) % values.shape[longest]
        spots.append(tuple(where))
    return values.at[spots[0]].set(least).at[spots[1]].set(largest)


def with_spikes(entries, own_key, source, target, shards_of, factor):
    owner, partner = [(jnp.arange(entries.shape[position]) // (entries.shape[position] // shards_of)).reshape([-1 if axis == position else 1 for axis in range(entries.ndim)]) for position in (source, target)]
    chosen = jax.random.permutation(own_key, shards_of)[partner]
    strong = (owner == chosen) | (owner == (partner + shards_of // 2) % shards_of)
    return jnp.where(strong, factor * entries, entries)


def shard_levels(stream_key, dims, cuts, least, high):
    gain = 1.0
    for dim, blocks in cuts:
        heights = jax.random.uniform(jax.random.fold_in(jax.random.fold_in(stream_key, 6), dim), (blocks,), jnp.float32, least / len(cuts), high / len(cuts))
        gain = gain * jnp.repeat(jnp.exp(heights), dims[dim] // blocks).reshape((-1,) + (1,) * (len(dims) - 1 - dim))
    return gain


def noise(stream_key, shape, deviation, bound, shards=(), kind=jnp.bfloat16):
    array = jax.random.normal(stream_key, shape, jnp.float32) * deviation
    if len(shards) > 0:
        array = shard_levels(stream_key, shape, shards, -0.22, 0.18) * array
    return jnp.clip(array, min=-bound, max=bound).astype(kind)


def gaussian_with(own_key, shape, scale, limit, pieces, heavy, held_as=jnp.bfloat16):
    values = scale * jax.random.normal(own_key, shape, jnp.float32)
    if pieces:
        values = values * shard_levels(own_key, shape, pieces, -0.22, 0.18)
    return jnp.clip(with_spikes(values, jax.random.fold_in(own_key, 3), *heavy), -limit, limit).astype(held_as)


def setup_inputs(seed: int = 0) -> dict:
    key_of = jax.random.split(jax.random.key(seed), 11)
    features = noise(key_of[0], (N_GRP * N_REP * ROWS_DEV, FEAT), 1.0, 6.0, ((0, 32),))
    fetch_row = place_ends(jax.random.randint(key_of[1], (N_GRP * N_GRP, N_REP * SLOTS), 0, ROWS_DEV), jax.random.fold_in(key_of[1], 1), 0, ROWS_DEV - 1).astype(jnp.int32)
    live_count = draw_live_count(jax.random.fold_in(key_of[10], 71), 0)
    seed_features = noise(key_of[3], (SEEDS, FEAT), 1.0, 6.0, ((0, 32),))
    tile_block = jax.vmap(lambda own: jax.random.permutation(own, FETCH // 128))(jax.random.split(key_of[4], (SEEDS // 128))).reshape((SEEDS // 128, FETCH // 128)).astype(jnp.int32)
    tile_weight = noise(key_of[5], (SEEDS // 128, FETCH // 128, 128, 128), FETCH ** -0.5, 0.375, ((0, 32),))
    self_weight = noise(key_of[6], (FEAT, HID), FEAT ** -0.5, 0.21875)
    neighbour_weight = noise(key_of[7], (FEAT, HID), FEAT ** -0.5, 0.21875)
    layer_bias = noise(key_of[8], (HID,), 1.0, 4.0, (), jnp.float32)
    cotangent = gaussian_with(key_of[9], (SEEDS, HID), 1.0, 6.0, ((0, 32),), (0, 1, 32, 2.75))
    return {"features": features, "fetch_row": fetch_row, "live_count": live_count, "seed_features": seed_features, "tile_block": tile_block, "tile_weight": tile_weight, "self_weight": self_weight, "neighbour_weight": neighbour_weight, "layer_bias": layer_bias, "cotangent": cotangent}


def reference(features, fetch_row, live_count, seed_features, tile_block, tile_weight, self_weight, neighbour_weight, layer_bias, cotangent):
    devices = N_GRP * N_REP
    fetch_blocks = N_GRP * SLOTS // 128
    seed_blocks = TGT // 128
    tables = features.reshape(N_GRP, N_REP, ROWS_DEV, FEAT)
    asked_all = fetch_row.reshape(N_GRP, N_GRP, N_REP, SLOTS)
    counts_all = live_count.reshape(N_GRP, N_GRP, N_REP)
    seeds_all = seed_features.reshape(devices, TGT, FEAT)
    block_all = tile_block.reshape(devices, seed_blocks, fetch_blocks)
    edges_all = tile_weight.reshape(devices, seed_blocks, fetch_blocks, 128, 128)
    cot_all = cotangent.reshape(devices, TGT, HID)
    peer_ix = jnp.arange(N_GRP, dtype=jnp.int32)
    slot_ix = jnp.arange(SLOTS, dtype=jnp.int32)
    self_f = self_weight.astype(jnp.float32)
    neigh_f = neighbour_weight.astype(jnp.float32)

    def accumulate(device, total):
        group_ix = device // N_REP
        rep_ix = device % N_REP
        asked = asked_all[group_ix, :, rep_ix, :]
        owner_tables = tables[:, rep_ix]
        table_rows = owner_tables[peer_ix[:, None], asked]
        live_mask = slot_ix[None, :] < counts_all[group_ix, :, rep_ix][:, None]
        table_rows = jnp.where(live_mask[:, :, None], table_rows, jnp.zeros((), jnp.bfloat16))
        row_blocks = table_rows.reshape(fetch_blocks, 128, FEAT)
        chosen = row_blocks[block_all[device]]
        aggregated = jnp.einsum("bkij,bkjf->bif", edges_all[device].astype(jnp.float32), chosen.astype(jnp.float32))
        aggregated = aggregated.reshape(TGT, FEAT).astype(jnp.bfloat16)
        seeds = seeds_all[device]
        pre_act = jnp.dot(seeds.astype(jnp.float32), self_f, preferred_element_type=jnp.float32)
        pre_act = pre_act + jnp.dot(aggregated.astype(jnp.float32), neigh_f, preferred_element_type=jnp.float32)
        pre_act = pre_act + layer_bias.astype(jnp.float32)[None, :]
        sigmoid_val = jax.nn.sigmoid(pre_act)
        slope = sigmoid_val * (1.0 + pre_act * (1.0 - sigmoid_val))
        grad_pre = (cot_all[device].astype(jnp.float32) * slope).astype(jnp.bfloat16)
        term = lax.dot_general(grad_pre.astype(jnp.float32), aggregated.astype(jnp.float32), (((0,), (0,)), ((), ())), preferred_element_type=jnp.float32)
        return total + term

    start_total = jnp.zeros((HID, FEAT), jnp.float32)
    return lax.fori_loop(0, devices, accumulate, start_total)
```

```python
import functools

import jax
import jax.numpy as jnp
from jax import lax
from jax.experimental import pallas as pl
from jax.experimental.pallas import tpu as pltpu
from jax.sharding import PartitionSpec as P

MESH = pl.DeviceIdType.MESH
BF16 = jnp.bfloat16
F32 = jnp.float32


def dot(a, b, ca=1, cb=0):
    return lax.dot_general(a, b, (((ca,), (cb,)), ((), ())), preferred_element_type=F32)


def kernel(
    feat_hbm, row_hbm, live_hbm, seed_hbm, block_hbm, tile_hbm, self_hbm, neigh_hbm, bias_hbm, cot_hbm,
    out_ref,
    feat, row, live, seeds, block, tile, w_self, w_neigh, bias, cot,
    request, asked, table_rows, fetched, mixed, hidden,
    send_c, recv_c, own, send_1, recv_1, send_2, recv_2, send_3, recv_3,
    load_sem, ask_send, ask_recv, row_send, row_recv,
    c_send, c_recv, s1_send, s1_recv, s2_send, s2_recv, s3_send, s3_recv,
):
    g, r = lax.axis_index("grp"), lax.axis_index("rep")
    x, c = g // 2, g % 2
    z, y = r // 2, r % 2
    n_z = send_3.shape[0]
    part = send_3.shape[2]
    slots = row.shape[1]
    sib, x_near, x_far = x * 2 + (1 - c), (1 - x) * 2 + c, (1 - x) * 2 + (1 - c)
    group = (x_near, x_far, sib)
    y_near = z * 2 + (1 - y)

    def at(grp, rep):
        return {"grp": grp, "rep": rep}

    loads = []
    for k, (src, dst) in enumerate((
        (row_hbm, row), (live_hbm, live), (feat_hbm, feat), (seed_hbm, seeds), (self_hbm, w_self),
        (block_hbm, block), (tile_hbm, tile), (neigh_hbm, w_neigh), (bias_hbm, bias), (cot_hbm, cot),
    )):
        load = pltpu.make_async_copy(src, dst, load_sem.at[k])
        load.start()
        loads.append(load)

    barrier = pltpu.get_barrier_semaphore()
    for peer in group:
        pl.semaphore_signal(barrier, inc=1, device_id=at(peer, r), device_id_type=MESH)
    pl.semaphore_signal(barrier, inc=1, device_id=at(g, y_near), device_id_type=MESH)
    for d in range(1, n_z):
        pl.semaphore_signal(barrier, inc=1, device_id=at(g, (z + d) % n_z * 2 + y), device_id_type=MESH)

    loads[0].wait()
    loads[1].wait()
    slot_ix = lax.broadcasted_iota(jnp.int32, row.shape, 1)
    wanted = jnp.where(slot_ix < live[...], row[...], -1)
    for p in range(4):
        line = jnp.broadcast_to(wanted[p : p + 1, :], (8, slots))
        request[p, :, 0:slots] = line
        request[p, :, slots : 2 * slots] = line
    pl.semaphore_wait(barrier, 3 + n_z)

    asks = []
    for k, peer in enumerate(group):
        copy = pltpu.make_async_remote_copy(
            src_ref=request.at[peer], dst_ref=asked.at[g], send_sem=ask_send.at[k], recv_sem=ask_recv.at[k],
            device_id=at(peer, r), device_id_type=MESH,
        )
        copy.start()
        asks.append(copy)
    asked[g] = request[g]
    loads[2].wait()

    def gather(chip):
        lane = lax.broadcasted_iota(jnp.int32, (1, 2 * slots), 1)
        ix = jnp.where(lane < slots, asked[2 * chip][0:1, :], asked[2 * chip + 1][0:1, :])
        rows_ix = lax.broadcasted_iota(jnp.int32, (feat.shape[0], 2 * slots), 0)
        pick = jnp.where(rows_ix == ix, 1.0, 0.0).astype(BF16)
        rows = dot(pick, feat[...], 0, 0).astype(BF16)
        table_rows[2 * chip] = rows[0:slots]
        table_rows[2 * chip + 1] = rows[slots : 2 * slots]

    def row_copy(k):
        return pltpu.make_async_remote_copy(
            src_ref=table_rows.at[group[k]], dst_ref=fetched.at[g], send_sem=row_send.at[k],
            recv_sem=row_recv.at[k], device_id=at(group[k], r), device_id_type=MESH,
        )

    asks[0].wait()
    asks[1].wait()
    gather(1 - x)
    rows_out = [row_copy(0), row_copy(1), row_copy(2)]
    rows_out[0].start()
    rows_out[1].start()
    asks[2].wait()
    gather(x)
    rows_out[2].start()
    fetched[g] = table_rows[g]

    loads[3].wait()
    loads[4].wait()
    hidden[...] = dot(seeds[...], w_self[...])
    for k in range(5, 10):
        loads[k].wait()
    n_b, n_k, rows_b, cols_b = tile.shape
    order = block[...]
    for b in range(n_b):
        for j in range(n_k):
            total = jnp.zeros((rows_b, cols_b), F32)
            for k in range(n_k):
                here = jnp.broadcast_to(order[b : b + 1, k : k + 1], (rows_b, cols_b)) == j
                total = jnp.where(here, tile[b, k].astype(F32), total)
            mixed[b * rows_b : (b + 1) * rows_b, j * cols_b : (j + 1) * cols_b] = total.astype(BF16)
    hidden[...] += bias[...]
    for copy in rows_out:
        copy.wait()

    rows_in = fetched[...].reshape(4 * slots, fetched.shape[2])
    agg = dot(mixed[...], rows_in).astype(BF16)
    pre = hidden[...] + dot(agg, w_neigh[...])
    sig = 0.5 * jnp.tanh(0.5 * pre) + 0.5
    grad = (cot[...].astype(F32) * (sig * (1.0 + pre * (1.0 - sig)))).astype(BF16)
    lanes = own.shape[-1]

    def half(core):
        cols = [grad[:, (2 * k) * lanes : (2 * k + 1) * lanes] for k in range(2)]
        cols_1 = [grad[:, (2 * k + 1) * lanes : (2 * k + 2) * lanes] for k in range(2)]
        first, second = jnp.concatenate(cols, axis=1), jnp.concatenate(cols_1, axis=1)
        return dot(agg, jnp.where(core == 0, first, second), 0, 0)

    def scatter(ref, value, kind):
        for rep in range(2 * n_z):
            rz, ry = rep // 2, rep % 2
            for h in range(2):
                lo = rep * 2 * part + h * part
                for rx in range(2):
                    piece = value[lo : lo + part, rx * lanes : (rx + 1) * lanes].astype(kind)
                    ref[(h,) + ((rx, ry) if h == 0 else (ry, rx)) + (rz,)] = piece

    scatter(send_c, half(1 - c), BF16)
    core_out = []
    for h in range(2):
        copy = pltpu.make_async_remote_copy(
            src_ref=send_c.at[h], dst_ref=recv_c.at[h], send_sem=c_send.at[h], recv_sem=c_recv.at[h],
            device_id=at(sib, r), device_id_type=MESH,
        )
        copy.start()
        core_out.append(copy)
    scatter(own, half(c), F32)

    near = (at(x_near, r), at(g, y_near))
    place = (x, y)
    outs_1 = []
    for h in range(2):
        core_out[h].wait()
        i = place[h]
        send_1[h] = (own[h, 1 - i] + recv_c[h, 1 - i].astype(F32)).astype(BF16)
        copy = pltpu.make_async_remote_copy(
            src_ref=send_1.at[h], dst_ref=recv_1.at[h], send_sem=s1_send.at[h], recv_sem=s1_recv.at[h],
            device_id=near[h], device_id_type=MESH,
        )
        copy.start()
        outs_1.append(copy)
    for h in range(2):
        i = place[h]
        own[h, i] = own[h, i] + recv_c[h, i].astype(F32)
    outs_2 = []
    for h in range(2):
        outs_1[h].wait()
        i, j = place[h], place[1 - h]
        send_2[h] = (own[h, i, 1 - j] + recv_1[h, 1 - j].astype(F32)).astype(BF16)
        copy = pltpu.make_async_remote_copy(
            src_ref=send_2.at[h], dst_ref=recv_2.at[h], send_sem=s2_send.at[h], recv_sem=s2_recv.at[h],
            device_id=near[1 - h], device_id_type=MESH,
        )
        copy.start()
        outs_2.append(copy)
    for h in range(2):
        i, j = place[h], place[1 - h]
        own[h, i, j] = own[h, i, j] + recv_1[h, j].astype(F32)
    for h in range(2):
        outs_2[h].wait()
        i, j = place[h], place[1 - h]
        done = own[h, i, j] + recv_2[h].astype(F32)
        own[h, i, j] = done
        for rz in range(n_z):
            send_3[rz, h] = done[rz].astype(BF16)
    outs_3 = []
    for d in range(1, n_z):
        to = (z + d) % n_z
        copy = pltpu.make_async_remote_copy(
            src_ref=send_3.at[to], dst_ref=recv_3.at[d - 1], send_sem=s3_send.at[d - 1],
            recv_sem=s3_recv.at[d - 1], device_id=at(g, to * 2 + y), device_id_type=MESH,
        )
        copy.start()
        outs_3.append(copy)
    total = jnp.concatenate([own[h, place[h], place[1 - h], z] for h in range(2)], axis=0)
    for copy in outs_3:
        copy.wait()
    for d in range(n_z - 1):
        total = total + recv_3[d].astype(F32).reshape(total.shape)
    out_ref[...] = total.T


def fused(features, fetch_row, live_count, seed_features, tile_block, tile_weight, self_weight, neighbour_weight, layer_bias, cotangent):
    width, hid = neighbour_weight.shape
    seeds = seed_features.shape[0]
    slots = fetch_row.shape[1]
    n_z = 4
    lanes = hid // 4
    part = width // (4 * n_z)
    bias = layer_bias.reshape(1, hid)
    operands = (features, fetch_row, live_count, seed_features, tile_block, tile_weight, self_weight, neighbour_weight, bias, cotangent)
    n_b, n_k, rows_b, cols_b = tile_weight.shape
    vmem = pltpu.VMEM
    dma = pltpu.SemaphoreType.DMA
    return pl.pallas_call(
        kernel,
        out_shape=jax.ShapeDtypeStruct((lanes, width // (2 * n_z)), F32),
        in_specs=[pl.BlockSpec(memory_space=pl.ANY)] * len(operands),
        out_specs=pl.BlockSpec(memory_space=vmem),
        scratch_shapes=[vmem(a.shape, a.dtype) for a in operands] + [
            vmem((4, 8, 2 * slots), jnp.int32),
            vmem((4, 8, 2 * slots), jnp.int32),
            vmem((4, slots, width), BF16),
            vmem((4, slots, width), BF16),
            vmem((seeds, n_k * cols_b), BF16),
            vmem((seeds, hid), F32),
            vmem((2, 2, 2, n_z, part, lanes), BF16),
            vmem((2, 2, 2, n_z, part, lanes), BF16),
            vmem((2, 2, 2, n_z, part, lanes), F32),
            vmem((2, 2, n_z, part, lanes), BF16),
            vmem((2, 2, n_z, part, lanes), BF16),
            vmem((2, n_z, part, lanes), BF16),
            vmem((2, n_z, part, lanes), BF16),
            vmem((n_z, 2, part, lanes), BF16),
            vmem((n_z - 1, 2, part, lanes), BF16),
            dma((10,)), dma((3,)), dma((3,)), dma((3,)), dma((3,)),
            dma((2,)), dma((2,)), dma((2,)), dma((2,)), dma((2,)), dma((2,)), dma((n_z - 1,)), dma((n_z - 1,)),
        ],
        compiler_params=pltpu.CompilerParams(
            collective_id=0, has_side_effects=True, vmem_limit_bytes=48 * 1024 * 1024
        ),
        name="sage_step",
    )(*operands)


def plain(
    features,
    fetch_row,
    live_count,
    seed_features,
    tile_block,
    tile_weight,
    self_weight,
    neighbour_weight,
    layer_bias,
    cotangent,
):
    width = features.shape[1]
    asked = lax.all_to_all(fetch_row, "grp", split_axis=0, concat_axis=0, tiled=True)
    table_rows = jnp.take(features, asked.reshape(-1), axis=0).reshape(asked.shape + (width,))
    fetched = lax.all_to_all(table_rows, "grp", split_axis=0, concat_axis=0, tiled=True)
    live_mask = lax.broadcasted_iota(jnp.int32, fetch_row.shape, 1) < live_count
    fetched = jnp.where(live_mask[:, :, None], fetched, jnp.zeros((), fetched.dtype))
    row_blocks = fetched.reshape(-1, 128, width)
    chosen = jnp.take(row_blocks, tile_block, axis=0)
    aggregated = jnp.einsum(
        "bkij,bkjf->bif", tile_weight, chosen, preferred_element_type=jnp.float32
    )
    aggregated = aggregated.reshape(-1, width).astype(jnp.bfloat16)
    pre_act = jnp.dot(seed_features, self_weight, preferred_element_type=jnp.float32)
    pre_act = pre_act + jnp.dot(aggregated, neighbour_weight, preferred_element_type=jnp.float32)
    pre_act = pre_act + layer_bias[None, :]
    sigmoid_val = jax.nn.sigmoid(pre_act)
    slope = sigmoid_val * (1.0 + pre_act * (1.0 - sigmoid_val))
    grad_pre = (cotangent.astype(jnp.float32) * slope).astype(jnp.bfloat16)
    partial_sum = lax.psum_scatter(
        lax.dot_general(
            grad_pre, aggregated, (((0,), (0,)), ((), ())), preferred_element_type=jnp.float32
        ),
        "grp",
        scatter_dimension=0,
        tiled=True,
    )
    return lax.psum_scatter(partial_sum, "rep", scatter_dimension=1, tiled=True)


def solution(mesh):
    placed = (
        P(("grp", "rep"), None),
        P("grp", "rep"),
        P("grp", "rep"),
        P(("grp", "rep"), None),
        P(("grp", "rep"), None),
        P(("grp", "rep"), None, None, None),
        P(),
        P(),
        P(),
        P(("grp", "rep"), None),
    )
    body = fused if (mesh.shape["grp"], mesh.shape["rep"]) == (4, 8) else plain
    return jax.shard_map(
        body, mesh=mesh, in_specs=placed, out_specs=P("grp", "rep"), check_vma=False
    )
```

```python
import functools

import jax
import jax.numpy as jnp
from jax import lax
from jax.experimental import pallas as pl
from jax.experimental.pallas import tpu as pltpu
from jax.sharding import PartitionSpec as P

MESH = pl.DeviceIdType.MESH
BF16 = jnp.bfloat16
F32 = jnp.float32


def dot(a, b, ca=1, cb=0):
    return lax.dot_general(a, b, (((ca,), (cb,)), ((), ())), preferred_element_type=F32)


def kernel(
    feat_hbm, row_hbm, live_hbm, seed_hbm, block_hbm, tile_hbm, self_hbm, neigh_hbm, bias_hbm, cot_hbm,
    out_ref,
    feat, row, live, seeds, block, tile, w_self, w_neigh, bias, cot,
    request, asked, table_rows, fetched, mixed, hidden, agg_t,
    send_c, recv_c, own, send_1, recv_1, send_2, recv_2, send_3, recv_3,
    load_sem, ask_send, ask_recv, row_send, row_recv,
    c_send, c_recv, s1_send, s1_recv, s2_send, s2_recv, s3_send, s3_recv,
):
    g, r = lax.axis_index("grp"), lax.axis_index("rep")
    x, c = g // 2, g % 2
    z, y = r // 2, r % 2
    n_z = recv_3.shape[0] + 1
    slots = row.shape[1]
    lanes, part = own.shape[-1], own.shape[-2]
    n_f, width_f = fetched.shape[0], fetched.shape[3]
    sib, x_near, x_far = x * 2 + (1 - c), (1 - x) * 2 + c, (1 - x) * 2 + (1 - c)
    group = (x_near, x_far, sib)
    y_near = z * 2 + (1 - y)

    def at(grp, rep):
        return {"grp": grp, "rep": rep}

    barrier = pltpu.get_barrier_semaphore()
    for peer in group:
        pl.semaphore_signal(barrier, inc=1, device_id=at(peer, r), device_id_type=MESH)
    pl.semaphore_signal(barrier, inc=1, device_id=at(g, y_near), device_id_type=MESH)
    for d in range(1, n_z):
        pl.semaphore_signal(barrier, inc=1, device_id=at(g, (z + d) % n_z * 2 + y), device_id_type=MESH)

    loads = {}

    def load(name, src, dst):
        copy = pltpu.make_async_copy(src, dst, load_sem.at[sum(len(v) for v in loads.values())])
        copy.start()
        loads.setdefault(name, []).append(copy)

    def ready(*names):
        for name in names:
            for copy in loads[name]:
                copy.wait()

    hidden_order = (x_far, sib, x_near, g)

    def load_hidden(name, src, dst):
        for k, unit in enumerate(hidden_order):
            cols = pl.ds(pl.multiple_of(unit * lanes, lanes), lanes)
            load(name, src.at[:, cols], dst.at[:, k * lanes : (k + 1) * lanes])

    load("ask", row_hbm, row)
    load("ask", live_hbm, live)
    load("feat", feat_hbm, feat)
    load("seeds", seed_hbm, seeds)
    load_hidden("self", self_hbm, w_self)
    load("tile", block_hbm, block)
    load("tile", tile_hbm, tile)
    load_hidden("bias", bias_hbm, bias)
    load_hidden("neigh", neigh_hbm, w_neigh)
    load_hidden("cot", cot_hbm, cot)

    ready("ask")
    slot_ix = lax.broadcasted_iota(jnp.int32, (1, slots), 1)
    for p in range(4):
        line = jnp.where(slot_ix < live[0:1, p : p + 1], row[p : p + 1, :], -1)
        line = jnp.broadcast_to(line, (8, slots))
        request[p, :, 0:slots] = line
        request[p, :, slots : 2 * slots] = line
    pl.semaphore_wait(barrier, 3 + n_z)

    asks = []
    for k, peer in enumerate(group):
        copy = pltpu.make_async_remote_copy(
            src_ref=request.at[peer], dst_ref=asked.at[g], send_sem=ask_send.at[k], recv_sem=ask_recv.at[k],
            device_id=at(peer, r), device_id_type=MESH,
        )
        copy.start()
        asks.append(copy)
    asked[g] = request[g]
    ready("feat")

    def picks(chip):
        lane = lax.broadcasted_iota(jnp.int32, (1, 2 * slots), 1)
        ix = jnp.where(lane < slots, asked[2 * chip][0:1, :], asked[2 * chip + 1][0:1, :])
        rows_ix = lax.broadcasted_iota(jnp.int32, (feat.shape[0], 2 * slots), 0)
        return jnp.where(rows_ix == ix, 1.0, 0.0).astype(BF16).T

    def gather(pick, chip, f):
        rows = dot(pick, feat[:, f * width_f : (f + 1) * width_f]).astype(BF16)
        table_rows[f, 2 * chip] = rows[0:slots]
        table_rows[f, 2 * chip + 1] = rows[slots : 2 * slots]

    rows_out = {}

    def send_rows(k, f):
        copy = pltpu.make_async_remote_copy(
            src_ref=table_rows.at[f, group[k]], dst_ref=fetched.at[f, g], send_sem=row_send.at[f, k],
            recv_sem=row_recv.at[f, k], device_id=at(group[k], r), device_id_type=MESH,
        )
        copy.start()
        rows_out[f, k] = copy

    asks[0].wait()
    asks[1].wait()
    pick = picks(1 - x)
    for f in range(n_f):
        gather(pick, 1 - x, f)
        send_rows(0, f)
        send_rows(1, f)
    asks[2].wait()
    pick = picks(x)
    for f in range(n_f):
        gather(pick, x, f)
        send_rows(2, f)
        fetched[f, g] = table_rows[f, g]

    ready("seeds", "self")
    hidden[...] = dot(seeds[...], w_self[...])
    ready("tile")
    n_b, n_k, rows_b, cols_b = tile.shape
    order = block[...]
    for b in range(n_b):
        for j in range(n_k):
            total = jnp.zeros((rows_b, cols_b), F32)
            for k in range(n_k):
                here = jnp.broadcast_to(order[k : k + 1, b : b + 1], (rows_b, cols_b)) == j
                total = jnp.where(here, tile[b, k].astype(F32), total)
            mixed[b * rows_b : (b + 1) * rows_b, j * cols_b : (j + 1) * cols_b] = total.astype(BF16)
    ready("bias", "neigh", "cot")
    hidden[...] += bias[...]

    for f in range(n_f):
        for k in range(3):
            rows_out[f, k].wait()
        cols = slice(f * width_f, (f + 1) * width_f)
        agg = dot(mixed[...], fetched[f].reshape(4 * slots, width_f)).astype(BF16)
        if f < n_f - 1:
            hidden[...] += dot(agg, w_neigh[cols, :])
        agg_t[cols, :] = agg.T

    def grad(side):
        units = slice(side * 2 * lanes, (side + 1) * 2 * lanes)
        pre = hidden[:, units] + dot(agg, w_neigh[cols, units])
        sig = 0.5 * jnp.tanh(0.5 * pre) + 0.5
        return (cot[:, units].astype(F32) * (sig * (1.0 + pre * (1.0 - sig)))).astype(BF16)

    offsets = ((2, 1), (3, 0))

    def weight_part(grad_side, q, ref, kind):
        lhs = []
        for d in offsets[q]:
            for rep_y in (1 - y, y):
                first = pl.multiple_of(((z + d) % n_z * 2 + rep_y) * 2 * part, 2 * part)
                lhs.append(agg_t[pl.ds(first, 2 * part), :])
        value = dot(jnp.concatenate(lhs, axis=0), grad_side)
        for dd in range(2):
            for ry in range(2):
                for h in range(2):
                    lo = ((dd * 2 + ry) * 2 + h) * part
                    for rx in range(2):
                        piece = value[lo : lo + part, rx * lanes : (rx + 1) * lanes].astype(kind)
                        ref[(q, h) + ((rx, ry) if h == 0 else (ry, rx)) + (dd,)] = piece

    def exchange(src, dst, sends, recvs, peer):
        copy = pltpu.make_async_remote_copy(
            src_ref=src, dst_ref=dst, send_sem=sends, recv_sem=recvs, device_id=peer, device_id_type=MESH
        )
        copy.start()
        return copy

    near = (at(x_near, r), at(g, y_near))
    core_out, outs_1, outs_2, outs_3 = [], {}, {}, []
    grad_side = grad(0)
    for q in range(2):
        weight_part(grad_side, q, send_c, BF16)
        core_out.append(exchange(send_c.at[q], recv_c.at[q], c_send.at[q], c_recv.at[q], at(sib, r)))
    grad_side = grad(1)
    for q in range(2):
        weight_part(grad_side, q, own, F32)
        core_out[q].wait()
        for h in range(2):
            send_1[q, h] = (own[q, h, 0] + recv_c[q, h, 0].astype(F32)).astype(BF16)
            outs_1[q, h] = exchange(send_1.at[q, h], recv_1.at[q, h], s1_send.at[q, h], s1_recv.at[q, h], near[h])
    for q in range(2):
        for h in range(2):
            kept = own[q, h, 1] + recv_c[q, h, 1].astype(F32)
            outs_1[q, h].wait()
            kept = kept + recv_1[q, h].astype(F32)
            send_2[q, h] = kept[0].astype(BF16)
            outs_2[q, h] = exchange(send_2.at[q, h], recv_2.at[q, h], s2_send.at[q, h], s2_recv.at[q, h], near[1 - h])
            own[q, h, 1, 1] = kept[1]
    for q in range(2):
        for h in range(2):
            outs_2[q, h].wait()
            for dd, d in enumerate(offsets[q]):
                done = own[q, h, 1, 1, dd] + recv_2[q, h, dd].astype(F32)
                if d > 0:
                    send_3[d - 1, h] = done.astype(BF16)
                else:
                    own[q, h, 1, 1, dd] = done
        for d in offsets[q]:
            if d > 0:
                to = at(g, (z + d) % n_z * 2 + y)
                outs_3.append(exchange(send_3.at[d - 1], recv_3.at[d - 1], s3_send.at[d - 1], s3_recv.at[d - 1], to))
    total = jnp.concatenate([own[1, h, 1, 1, 1] for h in range(2)], axis=0)
    for copy in outs_3:
        copy.wait()
    for d in range(n_z - 1):
        total = total + recv_3[d].astype(F32).reshape(total.shape)
    out_ref[...] = total


def fused(features, fetch_row, live_count, seed_features, tile_block, tile_weight, self_weight, neighbour_weight, layer_bias, cotangent):
    width, hid = neighbour_weight.shape
    seeds = seed_features.shape[0]
    slots = fetch_row.shape[1]
    n_z, n_f = 4, 3
    lanes = hid // 4
    part = width // (4 * n_z)
    bias = layer_bias.reshape(1, hid)
    operands = (features, fetch_row, live_count.T, seed_features, tile_block.T, tile_weight, self_weight, neighbour_weight, bias, cotangent)
    n_b, n_k, rows_b, cols_b = tile_weight.shape
    vmem = pltpu.VMEM
    dma = pltpu.SemaphoreType.DMA
    result = pl.pallas_call(
        kernel,
        out_shape=jax.ShapeDtypeStruct((width // (2 * n_z), lanes), F32),
        in_specs=[pl.BlockSpec(memory_space=pltpu.HBM)] * len(operands),
        out_specs=pl.BlockSpec(memory_space=vmem),
        scratch_shapes=[vmem(a.shape, a.dtype) for a in operands] + [
            vmem((4, 8, 2 * slots), jnp.int32),
            vmem((4, 8, 2 * slots), jnp.int32),
            vmem((n_f, 4, slots, width // n_f), BF16),
            vmem((n_f, 4, slots, width // n_f), BF16),
            vmem((seeds, n_k * cols_b), BF16),
            vmem((seeds, hid), F32),
            vmem((width, seeds), BF16),
            vmem((2, 2, 2, 2, 2, part, lanes), BF16),
            vmem((2, 2, 2, 2, 2, part, lanes), BF16),
            vmem((2, 2, 2, 2, 2, part, lanes), F32),
            vmem((2, 2, 2, 2, part, lanes), BF16),
            vmem((2, 2, 2, 2, part, lanes), BF16),
            vmem((2, 2, 2, part, lanes), BF16),
            vmem((2, 2, 2, part, lanes), BF16),
            vmem((n_z - 1, 2, part, lanes), BF16),
            vmem((n_z - 1, 2, part, lanes), BF16),
            dma((22,)), dma((3,)), dma((3,)), dma((n_f, 3)), dma((n_f, 3)),
            dma((2,)), dma((2,)), dma((2, 2)), dma((2, 2)), dma((2, 2)), dma((2, 2)), dma((n_z - 1,)), dma((n_z - 1,)),
        ],
        compiler_params=pltpu.CompilerParams(
            collective_id=0, has_side_effects=True, vmem_limit_bytes=56 * 1024 * 1024
        ),
        name="sage_step",
    )(*operands)
    return result.T


def plain(
    features,
    fetch_row,
    live_count,
    seed_features,
    tile_block,
    tile_weight,
    self_weight,
    neighbour_weight,
    layer_bias,
    cotangent,
):
    width = features.shape[1]
    asked = lax.all_to_all(fetch_row, "grp", split_axis=0, concat_axis=0, tiled=True)
    table_rows = jnp.take(features, asked.reshape(-1), axis=0).reshape(asked.shape + (width,))
    fetched = lax.all_to_all(table_rows, "grp", split_axis=0, concat_axis=0, tiled=True)
    live_mask = lax.broadcasted_iota(jnp.int32, fetch_row.shape, 1) < live_count
    fetched = jnp.where(live_mask[:, :, None], fetched, jnp.zeros((), fetched.dtype))
    row_blocks = fetched.reshape(-1, 128, width)
    chosen = jnp.take(row_blocks, tile_block, axis=0)
    aggregated = jnp.einsum(
        "bkij,bkjf->bif", tile_weight, chosen, preferred_element_type=jnp.float32
    )
    aggregated = aggregated.reshape(-1, width).astype(jnp.bfloat16)
    pre_act = jnp.dot(seed_features, self_weight, preferred_element_type=jnp.float32)
    pre_act = pre_act + jnp.dot(aggregated, neighbour_weight, preferred_element_type=jnp.float32)
    pre_act = pre_act + layer_bias[None, :]
    sigmoid_val = jax.nn.sigmoid(pre_act)
    slope = sigmoid_val * (1.0 + pre_act * (1.0 - sigmoid_val))
    grad_pre = (cotangent.astype(jnp.float32) * slope).astype(jnp.bfloat16)
    partial_sum = lax.psum_scatter(
        lax.dot_general(
            grad_pre, aggregated, (((0,), (0,)), ((), ())), preferred_element_type=jnp.float32
        ),
        "grp",
        scatter_dimension=0,
        tiled=True,
    )
    return lax.psum_scatter(partial_sum, "rep", scatter_dimension=1, tiled=True)


def solution(mesh):
    placed = (
        P(("grp", "rep"), None),
        P("grp", "rep"),
        P("grp", "rep"),
        P(("grp", "rep"), None),
        P(("grp", "rep"), None),
        P(("grp", "rep"), None, None, None),
        P(),
        P(),
        P(),
        P(("grp", "rep"), None),
    )
    body = fused if (mesh.shape["grp"], mesh.shape["rep"]) == (4, 8) else plain
    return jax.shard_map(
        body, mesh=mesh, in_specs=placed, out_specs=P("grp", "rep"), check_vma=False
    )
```

```python
import functools

import jax
import jax.numpy as jnp
from jax import lax
from jax.experimental import pallas as pl
from jax.experimental.pallas import tpu as pltpu
from jax.sharding import PartitionSpec as P

MESH = pl.DeviceIdType.MESH
BF16 = jnp.bfloat16
F32 = jnp.float32


def dot(a, b, ca=1, cb=0):
    return lax.dot_general(a, b, (((ca,), (cb,)), ((), ())), preferred_element_type=F32)


def kernel(
    feat_hbm, row_hbm, live_hbm, seed_hbm, block_hbm, tile_hbm, self_hbm, neigh_hbm, bias_hbm, cot_hbm,
    out_ref,
    feat, row, live, seeds, block, tile, w_self, w_neigh, bias, cot,
    request, asked, table_rows, fetched, mixed, hidden, agg_t,
    send_c, recv_c, own, send_1, recv_1, send_2, recv_2, send_3, recv_3,
    load_sem, ask_send, ask_recv, row_send, row_recv,
    c_send, c_recv, s1_send, s1_recv, s2_send, s2_recv, s3_send, s3_recv,
):
    g, r = lax.axis_index("grp"), lax.axis_index("rep")
    x, c = g // 2, g % 2
    z, y = r // 2, r % 2
    n_z = recv_3.shape[0] + 1
    slots = row.shape[1]
    lanes, part = own.shape[-1], own.shape[-2]
    n_f, width_f = fetched.shape[0], fetched.shape[3]
    sib, x_near, x_far = x * 2 + (1 - c), (1 - x) * 2 + c, (1 - x) * 2 + (1 - c)
    group = (x_near, x_far, sib)
    y_near = z * 2 + (1 - y)

    def at(grp, rep):
        return {"grp": grp, "rep": rep}

    barrier = pltpu.get_barrier_semaphore()
    for peer in group:
        pl.semaphore_signal(barrier, inc=1, device_id=at(peer, r), device_id_type=MESH)
    pl.semaphore_signal(barrier, inc=1, device_id=at(g, y_near), device_id_type=MESH)
    for d in range(1, n_z):
        pl.semaphore_signal(barrier, inc=1, device_id=at(g, (z + d) % n_z * 2 + y), device_id_type=MESH)

    loads = {}

    def load(name, src, dst):
        copy = pltpu.make_async_copy(src, dst, load_sem.at[sum(len(v) for v in loads.values())])
        copy.start()
        loads.setdefault(name, []).append(copy)

    def ready(*names):
        for name in names:
            for copy in loads[name]:
                copy.wait()

    hidden_order = (x_far, sib, x_near, g)

    def load_hidden(name, src, dst):
        for k, unit in enumerate(hidden_order):
            cols = pl.ds(pl.multiple_of(unit * lanes, lanes), lanes)
            load(name, src.at[:, cols], dst.at[:, k * lanes : (k + 1) * lanes])

    load("ask", row_hbm, row)
    load("ask", live_hbm, live)
    load("feat", feat_hbm, feat)

    ready("ask")
    slot_ix = lax.broadcasted_iota(jnp.int32, (1, slots), 1)
    for p in range(4):
        line = jnp.where(slot_ix < live[0:1, p : p + 1], row[p : p + 1, :], -1)
        line = jnp.broadcast_to(line, (8, slots))
        request[p, :, 0:slots] = line
        request[p, :, slots : 2 * slots] = line
    pl.semaphore_wait(barrier, 3 + n_z)

    asks = []
    for k, peer in enumerate(group):
        copy = pltpu.make_async_remote_copy(
            src_ref=request.at[peer], dst_ref=asked.at[g], send_sem=ask_send.at[k], recv_sem=ask_recv.at[k],
            device_id=at(peer, r), device_id_type=MESH,
        )
        copy.start()
        asks.append(copy)
    asked[g] = request[g]
    load("seeds", seed_hbm, seeds)
    load_hidden("self", self_hbm, w_self)
    load("tile", block_hbm, block)
    load("tile", tile_hbm, tile)
    load_hidden("bias", bias_hbm, bias)
    load_hidden("neigh", neigh_hbm, w_neigh)
    load_hidden("cot", cot_hbm, cot)
    ready("feat")

    def picks(chip):
        lane = lax.broadcasted_iota(jnp.int32, (1, 2 * slots), 1)
        ix = jnp.where(lane < slots, asked[2 * chip][0:1, :], asked[2 * chip + 1][0:1, :])
        rows_ix = lax.broadcasted_iota(jnp.int32, (feat.shape[0], 2 * slots), 0)
        return jnp.where(rows_ix == ix, 1.0, 0.0).astype(BF16).T

    def gather(pick, chip, f):
        rows = dot(pick, feat[:, f * width_f : (f + 1) * width_f]).astype(BF16)
        table_rows[f, 2 * chip] = rows[0:slots]
        table_rows[f, 2 * chip + 1] = rows[slots : 2 * slots]

    rows_out = {}

    def send_rows(k, f):
        copy = pltpu.make_async_remote_copy(
            src_ref=table_rows.at[f, group[k]], dst_ref=fetched.at[f, g], send_sem=row_send.at[f, k],
            recv_sem=row_recv.at[f, k], device_id=at(group[k], r), device_id_type=MESH,
        )
        copy.start()
        rows_out[f, k] = copy

    asks[0].wait()
    asks[1].wait()
    pick = picks(1 - x)
    for f in range(n_f):
        gather(pick, 1 - x, f)
        send_rows(0, f)
        send_rows(1, f)
    asks[2].wait()
    pick = picks(x)
    for f in range(n_f):
        gather(pick, x, f)
        send_rows(2, f)
        fetched[f, g] = table_rows[f, g]

    ready("seeds", "self")
    hidden[...] = dot(seeds[...], w_self[...])
    ready("tile")
    n_b, n_k, rows_b, cols_b = tile.shape
    order = block[...]
    for b in range(n_b):
        for j in range(n_k):
            total = jnp.zeros((rows_b, cols_b), F32)
            for k in range(n_k):
                here = jnp.broadcast_to(order[k : k + 1, b : b + 1], (rows_b, cols_b)) == j
                total = jnp.where(here, tile[b, k].astype(F32), total)
            mixed[b * rows_b : (b + 1) * rows_b, j * cols_b : (j + 1) * cols_b] = total.astype(BF16)
    ready("bias", "neigh", "cot")
    hidden[...] += bias[...]

    for f in range(n_f):
        for k in range(3):
            rows_out[f, k].wait()
        cols = slice(f * width_f, (f + 1) * width_f)
        agg = dot(mixed[...], fetched[f].reshape(4 * slots, width_f)).astype(BF16)
        if f < n_f - 1:
            hidden[...] += dot(agg, w_neigh[cols, :])
        agg_t[cols, :] = agg.T

    def grad(side):
        units = slice(side * 2 * lanes, (side + 1) * 2 * lanes)
        pre = hidden[:, units] + dot(agg, w_neigh[cols, units])
        sig = 0.5 * jnp.tanh(0.5 * pre) + 0.5
        return (cot[:, units].astype(F32) * (sig * (1.0 + pre * (1.0 - sig)))).astype(BF16)

    offsets = ((2, 1), (3, 0))

    def weight_part(grad_side, q, ref, kind):
        lhs = []
        for d in offsets[q]:
            for rep_y in (1 - y, y):
                first = pl.multiple_of(((z + d) % n_z * 2 + rep_y) * 2 * part, 2 * part)
                lhs.append(agg_t[pl.ds(first, 2 * part), :])
        value = dot(jnp.concatenate(lhs, axis=0), grad_side)
        for dd in range(2):
            for ry in range(2):
                for h in range(2):
                    lo = ((dd * 2 + ry) * 2 + h) * part
                    for rx in range(2):
                        piece = value[lo : lo + part, rx * lanes : (rx + 1) * lanes].astype(kind)
                        ref[(q, h) + ((rx, ry) if h == 0 else (ry, rx)) + (dd,)] = piece

    def exchange(src, dst, sends, recvs, peer):
        copy = pltpu.make_async_remote_copy(
            src_ref=src, dst_ref=dst, send_sem=sends, recv_sem=recvs, device_id=peer, device_id_type=MESH
        )
        copy.start()
        return copy

    near = (at(x_near, r), at(g, y_near))
    core_out, outs_1, outs_2, outs_3 = [], {}, {}, []
    grad_side = grad(0)
    for q in range(2):
        weight_part(grad_side, q, send_c, BF16)
        core_out.append(exchange(send_c.at[q], recv_c.at[q], c_send.at[q], c_recv.at[q], at(sib, r)))
    grad_side = grad(1)
    for q in range(2):
        weight_part(grad_side, q, own, F32)
        core_out[q].wait()
        for h in range(2):
            send_1[q, h] = (own[q, h, 0] + recv_c[q, h, 0].astype(F32)).astype(BF16)
            outs_1[q, h] = exchange(send_1.at[q, h], recv_1.at[q, h], s1_send.at[q, h], s1_recv.at[q, h], near[h])
    for q in range(2):
        for h in range(2):
            kept = own[q, h, 1] + recv_c[q, h, 1].astype(F32)
            outs_1[q, h].wait()
            kept = kept + recv_1[q, h].astype(F32)
            send_2[q, h] = kept[0].astype(BF16)
            outs_2[q, h] = exchange(send_2.at[q, h], recv_2.at[q, h], s2_send.at[q, h], s2_recv.at[q, h], near[1 - h])
            own[q, h, 1, 1] = kept[1]
    for q in range(2):
        for h in range(2):
            outs_2[q, h].wait()
            for dd, d in enumerate(offsets[q]):
                done = own[q, h, 1, 1, dd] + recv_2[q, h, dd].astype(F32)
                if d > 0:
                    send_3[d - 1, h] = done.astype(BF16)
                else:
                    own[q, h, 1, 1, dd] = done
        for d in offsets[q]:
            if d > 0:
                to = at(g, (z + d) % n_z * 2 + y)
                outs_3.append(exchange(send_3.at[d - 1], recv_3.at[d - 1], s3_send.at[d - 1], s3_recv.at[d - 1], to))
    total = jnp.concatenate([own[1, h, 1, 1, 1] for h in range(2)], axis=0)
    for copy in outs_3:
        copy.wait()
    for d in range(n_z - 1):
        total = total + recv_3[d].astype(F32).reshape(total.shape)
    out_ref[...] = total


def fused(features, fetch_row, live_count, seed_features, tile_block, tile_weight, self_weight, neighbour_weight, layer_bias, cotangent):
    width, hid = neighbour_weight.shape
    seeds = seed_features.shape[0]
    slots = fetch_row.shape[1]
    n_z, n_f = 4, 3
    lanes = hid // 4
    part = width // (4 * n_z)
    bias = layer_bias.reshape(1, hid)
    operands = (features, fetch_row, live_count.T, seed_features, tile_block.T, tile_weight, self_weight, neighbour_weight, bias, cotangent)
    n_b, n_k, rows_b, cols_b = tile_weight.shape
    vmem = pltpu.VMEM
    dma = pltpu.SemaphoreType.DMA
    result = pl.pallas_call(
        kernel,
        out_shape=jax.ShapeDtypeStruct((width // (2 * n_z), lanes), F32),
        in_specs=[pl.BlockSpec(memory_space=pltpu.HBM)] * len(operands),
        out_specs=pl.BlockSpec(memory_space=vmem),
        scratch_shapes=[vmem(a.shape, a.dtype) for a in operands] + [
            vmem((4, 8, 2 * slots), jnp.int32),
            vmem((4, 8, 2 * slots), jnp.int32),
            vmem((n_f, 4, slots, width // n_f), BF16),
            vmem((n_f, 4, slots, width // n_f), BF16),
            vmem((seeds, n_k * cols_b), BF16),
            vmem((seeds, hid), F32),
            vmem((width, seeds), BF16),
            vmem((2, 2, 2, 2, 2, part, lanes), BF16),
            vmem((2, 2, 2, 2, 2, part, lanes), BF16),
            vmem((2, 2, 2, 2, 2, part, lanes), F32),
            vmem((2, 2, 2, 2, part, lanes), BF16),
            vmem((2, 2, 2, 2, part, lanes), BF16),
            vmem((2, 2, 2, part, lanes), BF16),
            vmem((2, 2, 2, part, lanes), BF16),
            vmem((n_z - 1, 2, part, lanes), BF16),
            vmem((n_z - 1, 2, part, lanes), BF16),
            dma((22,)), dma((3,)), dma((3,)), dma((n_f, 3)), dma((n_f, 3)),
            dma((2,)), dma((2,)), dma((2, 2)), dma((2, 2)), dma((2, 2)), dma((2, 2)), dma((n_z - 1,)), dma((n_z - 1,)),
        ],
        compiler_params=pltpu.CompilerParams(
            collective_id=0, has_side_effects=True, vmem_limit_bytes=24 * 1024 * 1024
        ),
        name="sage_step",
    )(*operands)
    return result.T


def plain(
    features,
    fetch_row,
    live_count,
    seed_features,
    tile_block,
    tile_weight,
    self_weight,
    neighbour_weight,
    layer_bias,
    cotangent,
):
    width = features.shape[1]
    asked = lax.all_to_all(fetch_row, "grp", split_axis=0, concat_axis=0, tiled=True)
    table_rows = jnp.take(features, asked.reshape(-1), axis=0).reshape(asked.shape + (width,))
    fetched = lax.all_to_all(table_rows, "grp", split_axis=0, concat_axis=0, tiled=True)
    live_mask = lax.broadcasted_iota(jnp.int32, fetch_row.shape, 1) < live_count
    fetched = jnp.where(live_mask[:, :, None], fetched, jnp.zeros((), fetched.dtype))
    row_blocks = fetched.reshape(-1, 128, width)
    chosen = jnp.take(row_blocks, tile_block, axis=0)
    aggregated = jnp.einsum(
        "bkij,bkjf->bif", tile_weight, chosen, preferred_element_type=jnp.float32
    )
    aggregated = aggregated.reshape(-1, width).astype(jnp.bfloat16)
    pre_act = jnp.dot(seed_features, self_weight, preferred_element_type=jnp.float32)
    pre_act = pre_act + jnp.dot(aggregated, neighbour_weight, preferred_element_type=jnp.float32)
    pre_act = pre_act + layer_bias[None, :]
    sigmoid_val = jax.nn.sigmoid(pre_act)
    slope = sigmoid_val * (1.0 + pre_act * (1.0 - sigmoid_val))
    grad_pre = (cotangent.astype(jnp.float32) * slope).astype(jnp.bfloat16)
    partial_sum = lax.psum_scatter(
        lax.dot_general(
            grad_pre, aggregated, (((0,), (0,)), ((), ())), preferred_element_type=jnp.float32
        ),
        "grp",
        scatter_dimension=0,
        tiled=True,
    )
    return lax.psum_scatter(partial_sum, "rep", scatter_dimension=1, tiled=True)


def solution(mesh):
    placed = (
        P(("grp", "rep"), None),
        P("grp", "rep"),
        P("grp", "rep"),
        P(("grp", "rep"), None),
        P(("grp", "rep"), None),
        P(("grp", "rep"), None, None, None),
        P(),
        P(),
        P(),
        P(("grp", "rep"), None),
    )
    body = fused if (mesh.shape["grp"], mesh.shape["rep"]) == (4, 8) else plain
    return jax.shard_map(
        body, mesh=mesh, in_specs=placed, out_specs=P("grp", "rep"), check_vma=False
    )
```

```python
import functools

import jax
import jax.numpy as jnp
from jax import lax
from jax.experimental import pallas as pl
from jax.experimental.pallas import tpu as pltpu
from jax.sharding import PartitionSpec as P

MESH = pl.DeviceIdType.MESH
BF16 = jnp.bfloat16
F32 = jnp.float32


def dot(a, b, ca=1, cb=0):
    return lax.dot_general(a, b, (((ca,), (cb,)), ((), ())), preferred_element_type=F32)


def kernel(
    feat_hbm, row_hbm, live_hbm, seed_hbm, block_hbm, tile_hbm, self_hbm, neigh_hbm, bias_hbm, cot_hbm,
    out_ref,
    feat, row, live, seeds, block, tile, w_self, w_neigh, bias, cot,
    request, asked, table_rows, fetched, mixed, hidden, agg_t,
    send_c, recv_c, own, send_1, recv_1, send_2, recv_2, send_3, recv_3,
    load_sem, ask_send, ask_recv, row_send, row_recv,
    c_send, c_recv, s1_send, s1_recv, s2_send, s2_recv, s3_send, s3_recv,
):
    g, r = lax.axis_index("grp"), lax.axis_index("rep")
    x, c = g // 2, g % 2
    z, y = r // 2, r % 2
    n_z = recv_3.shape[0] + 1
    slots = row.shape[1]
    lanes, part = own.shape[-1], own.shape[-2]
    n_f, width_f = fetched.shape[0], fetched.shape[3]
    sib, x_near, x_far = x * 2 + (1 - c), (1 - x) * 2 + c, (1 - x) * 2 + (1 - c)
    group = (x_near, x_far, sib)
    y_near = z * 2 + (1 - y)

    def at(grp, rep):
        return {"grp": grp, "rep": rep}

    barrier = pltpu.get_barrier_semaphore()
    for peer in group:
        pl.semaphore_signal(barrier, inc=1, device_id=at(peer, r), device_id_type=MESH)
    pl.semaphore_signal(barrier, inc=1, device_id=at(g, y_near), device_id_type=MESH)
    for d in range(1, n_z):
        pl.semaphore_signal(barrier, inc=1, device_id=at(g, (z + d) % n_z * 2 + y), device_id_type=MESH)

    loads = {}

    def load(name, src, dst):
        copy = pltpu.make_async_copy(src, dst, load_sem.at[sum(len(v) for v in loads.values())])
        copy.start()
        loads.setdefault(name, []).append(copy)

    def ready(*names):
        for name in names:
            for copy in loads[name]:
                copy.wait()

    hidden_order = (x_far, sib, x_near, g)

    def load_hidden(name, src, dst):
        for k, unit in enumerate(hidden_order):
            cols = pl.ds(pl.multiple_of(unit * lanes, lanes), lanes)
            load(name, src.at[:, cols], dst.at[:, k * lanes : (k + 1) * lanes])

    load("ask", row_hbm, row)
    load("ask", live_hbm, live)
    load("feat", feat_hbm, feat)

    ready("ask")
    slot_ix = lax.broadcasted_iota(jnp.int32, (1, slots), 1)
    for p in range(4):
        line = jnp.where(slot_ix < live[0:1, p : p + 1], row[p : p + 1, :], -1)
        line = jnp.broadcast_to(line, (8, slots))
        request[p, :, 0:slots] = line
        request[p, :, slots : 2 * slots] = line
    pl.semaphore_wait(barrier, 3 + n_z)

    asks = []
    for k, peer in enumerate(group):
        copy = pltpu.make_async_remote_copy(
            src_ref=request.at[peer], dst_ref=asked.at[g], send_sem=ask_send.at[k], recv_sem=ask_recv.at[k],
            device_id=at(peer, r), device_id_type=MESH,
        )
        copy.start()
        asks.append(copy)
    asked[g] = request[g]
    load("seeds", seed_hbm, seeds)
    load_hidden("self", self_hbm, w_self)
    load("tile", block_hbm, block)
    load("tile", tile_hbm, tile)
    load_hidden("bias", bias_hbm, bias)
    load_hidden("neigh", neigh_hbm, w_neigh)
    load_hidden("cot", cot_hbm, cot)
    ready("feat")

    def picks(chip):
        lane = lax.broadcasted_iota(jnp.int32, (1, 2 * slots), 1)
        ix = jnp.where(lane < slots, asked[2 * chip][0:1, :], asked[2 * chip + 1][0:1, :])
        rows_ix = lax.broadcasted_iota(jnp.int32, (feat.shape[0], 2 * slots), 0)
        return jnp.where(rows_ix == ix, 1.0, 0.0).astype(BF16).T

    def gather(pick, chip, f):
        rows = dot(pick, feat[:, f * width_f : (f + 1) * width_f]).astype(BF16)
        table_rows[f, 2 * chip] = rows[0:slots]
        table_rows[f, 2 * chip + 1] = rows[slots : 2 * slots]

    rows_out = {}

    def send_rows(k, f):
        copy = pltpu.make_async_remote_copy(
            src_ref=table_rows.at[f, group[k]], dst_ref=fetched.at[f, g], send_sem=row_send.at[f, k],
            recv_sem=row_recv.at[f, k], device_id=at(group[k], r), device_id_type=MESH,
        )
        copy.start()
        rows_out[f, k] = copy

    asks[0].wait_recv()
    asks[1].wait_recv()
    pick = picks(1 - x)
    for f in range(n_f):
        gather(pick, 1 - x, f)
        send_rows(0, f)
        send_rows(1, f)
    asks[2].wait_recv()
    pick = picks(x)
    for f in range(n_f):
        gather(pick, x, f)
        send_rows(2, f)
        fetched[f, g] = table_rows[f, g]

    ready("seeds", "self")
    hidden[...] = dot(seeds[...], w_self[...])
    ready("tile")
    n_b, n_k, rows_b, cols_b = tile.shape
    order = block[...]
    for b in range(n_b):
        for j in range(n_k):
            total = jnp.zeros((rows_b, cols_b), F32)
            for k in range(n_k):
                here = jnp.broadcast_to(order[k : k + 1, b : b + 1], (rows_b, cols_b)) == j
                total = jnp.where(here, tile[b, k].astype(F32), total)
            mixed[b * rows_b : (b + 1) * rows_b, j * cols_b : (j + 1) * cols_b] = total.astype(BF16)
    ready("bias", "neigh", "cot")
    hidden[...] += bias[...]

    for f in range(n_f):
        for k in range(3):
            rows_out[f, k].wait_recv()
        cols = slice(f * width_f, (f + 1) * width_f)
        agg = dot(mixed[...], fetched[f].reshape(4 * slots, width_f)).astype(BF16)
        if f < n_f - 1:
            hidden[...] += dot(agg, w_neigh[cols, :])
        agg_t[cols, :] = agg.T

    def grad(side):
        units = slice(side * 2 * lanes, (side + 1) * 2 * lanes)
        pre = hidden[:, units] + dot(agg, w_neigh[cols, units])
        sig = 0.5 * jnp.tanh(0.5 * pre) + 0.5
        return (cot[:, units].astype(F32) * (sig * (1.0 + pre * (1.0 - sig)))).astype(BF16)

    offsets = ((2, 1), (3, 0))

    def weight_part(grad_side, q, ref, kind):
        lhs = []
        for d in offsets[q]:
            for rep_y in (1 - y, y):
                first = pl.multiple_of(((z + d) % n_z * 2 + rep_y) * 2 * part, 2 * part)
                lhs.append(agg_t[pl.ds(first, 2 * part), :])
        value = dot(jnp.concatenate(lhs, axis=0), grad_side)
        for dd in range(2):
            for ry in range(2):
                for h in range(2):
                    lo = ((dd * 2 + ry) * 2 + h) * part
                    for rx in range(2):
                        piece = value[lo : lo + part, rx * lanes : (rx + 1) * lanes].astype(kind)
                        ref[(q, h) + ((rx, ry) if h == 0 else (ry, rx)) + (dd,)] = piece

    def exchange(src, dst, sends, recvs, peer):
        copy = pltpu.make_async_remote_copy(
            src_ref=src, dst_ref=dst, send_sem=sends, recv_sem=recvs, device_id=peer, device_id_type=MESH
        )
        copy.start()
        return copy

    near = (at(x_near, r), at(g, y_near))
    core_out, outs_1, outs_2, outs_3 = [], {}, {}, []
    grad_side = grad(0)
    for q in range(2):
        weight_part(grad_side, q, send_c, BF16)
        core_out.append(exchange(send_c.at[q], recv_c.at[q], c_send.at[q], c_recv.at[q], at(sib, r)))
    grad_side = grad(1)
    for q in range(2):
        weight_part(grad_side, q, own, F32)
        core_out[q].wait_recv()
        for h in range(2):
            send_1[q, h] = (own[q, h, 0] + recv_c[q, h, 0].astype(F32)).astype(BF16)
            outs_1[q, h] = exchange(send_1.at[q, h], recv_1.at[q, h], s1_send.at[q, h], s1_recv.at[q, h], near[h])
    for q in range(2):
        for h in range(2):
            kept = own[q, h, 1] + recv_c[q, h, 1].astype(F32)
            outs_1[q, h].wait_recv()
            kept = kept + recv_1[q, h].astype(F32)
            send_2[q, h] = kept[0].astype(BF16)
            outs_2[q, h] = exchange(send_2.at[q, h], recv_2.at[q, h], s2_send.at[q, h], s2_recv.at[q, h], near[1 - h])
            own[q, h, 1, 1] = kept[1]
    for q in range(2):
        for h in range(2):
            outs_2[q, h].wait_recv()
            for dd, d in enumerate(offsets[q]):
                done = own[q, h, 1, 1, dd] + recv_2[q, h, dd].astype(F32)
                if d > 0:
                    send_3[d - 1, h] = done.astype(BF16)
                else:
                    own[q, h, 1, 1, dd] = done
        for d in offsets[q]:
            if d > 0:
                to = at(g, (z + d) % n_z * 2 + y)
                outs_3.append(exchange(send_3.at[d - 1], recv_3.at[d - 1], s3_send.at[d - 1], s3_recv.at[d - 1], to))
    total = jnp.concatenate([own[1, h, 1, 1, 1] for h in range(2)], axis=0)
    for copy in outs_3:
        copy.wait_recv()
    for d in range(n_z - 1):
        total = total + recv_3[d].astype(F32).reshape(total.shape)
    out_ref[...] = total
    for copies in (asks, rows_out.values(), core_out, outs_1.values(), outs_2.values(), outs_3):
        for copy in copies:
            copy.wait_send()


def fused(features, fetch_row, live_count, seed_features, tile_block, tile_weight, self_weight, neighbour_weight, layer_bias, cotangent):
    width, hid = neighbour_weight.shape
    seeds = seed_features.shape[0]
    slots = fetch_row.shape[1]
    n_z, n_f = 4, 3
    lanes = hid // 4
    part = width // (4 * n_z)
    bias = layer_bias.reshape(1, hid)
    operands = (features, fetch_row, live_count.T, seed_features, tile_block.T, tile_weight, self_weight, neighbour_weight, bias, cotangent)
    n_b, n_k, rows_b, cols_b = tile_weight.shape
    vmem = pltpu.VMEM
    dma = pltpu.SemaphoreType.DMA
    result = pl.pallas_call(
        kernel,
        out_shape=vmem((width // (2 * n_z), lanes), F32),
        in_specs=[pl.BlockSpec(memory_space=pltpu.HBM)] * len(operands),
        out_specs=pl.BlockSpec(memory_space=vmem),
        scratch_shapes=[vmem(a.shape, a.dtype) for a in operands] + [
            vmem((4, 8, 2 * slots), jnp.int32),
            vmem((4, 8, 2 * slots), jnp.int32),
            vmem((n_f, 4, slots, width // n_f), BF16),
            vmem((n_f, 4, slots, width // n_f), BF16),
            vmem((seeds, n_k * cols_b), BF16),
            vmem((seeds, hid), F32),
            vmem((width, seeds), BF16),
            vmem((2, 2, 2, 2, 2, part, lanes), BF16),
            vmem((2, 2, 2, 2, 2, part, lanes), BF16),
            vmem((2, 2, 2, 2, 2, part, lanes), F32),
            vmem((2, 2, 2, 2, part, lanes), BF16),
            vmem((2, 2, 2, 2, part, lanes), BF16),
            vmem((2, 2, 2, part, lanes), BF16),
            vmem((2, 2, 2, part, lanes), BF16),
            vmem((n_z - 1, 2, part, lanes), BF16),
            vmem((n_z - 1, 2, part, lanes), BF16),
            dma((22,)), dma((3,)), dma((3,)), dma((n_f, 3)), dma((n_f, 3)),
            dma((2,)), dma((2,)), dma((2, 2)), dma((2, 2)), dma((2, 2)), dma((2, 2)), dma((n_z - 1,)), dma((n_z - 1,)),
        ],
        compiler_params=pltpu.CompilerParams(
            collective_id=0, has_side_effects=True, vmem_limit_bytes=56 * 1024 * 1024
        ),
        name="sage_step",
    )(*operands)
    return result.T


def plain(
    features,
    fetch_row,
    live_count,
    seed_features,
    tile_block,
    tile_weight,
    self_weight,
    neighbour_weight,
    layer_bias,
    cotangent,
):
    width = features.shape[1]
    asked = lax.all_to_all(fetch_row, "grp", split_axis=0, concat_axis=0, tiled=True)
    table_rows = jnp.take(features, asked.reshape(-1), axis=0).reshape(asked.shape + (width,))
    fetched = lax.all_to_all(table_rows, "grp", split_axis=0, concat_axis=0, tiled=True)
    live_mask = lax.broadcasted_iota(jnp.int32, fetch_row.shape, 1) < live_count
    fetched = jnp.where(live_mask[:, :, None], fetched, jnp.zeros((), fetched.dtype))
    row_blocks = fetched.reshape(-1, 128, width)
    chosen = jnp.take(row_blocks, tile_block, axis=0)
    aggregated = jnp.einsum(
        "bkij,bkjf->bif", tile_weight, chosen, preferred_element_type=jnp.float32
    )
    aggregated = aggregated.reshape(-1, width).astype(jnp.bfloat16)
    pre_act = jnp.dot(seed_features, self_weight, preferred_element_type=jnp.float32)
    pre_act = pre_act + jnp.dot(aggregated, neighbour_weight, preferred_element_type=jnp.float32)
    pre_act = pre_act + layer_bias[None, :]
    sigmoid_val = jax.nn.sigmoid(pre_act)
    slope = sigmoid_val * (1.0 + pre_act * (1.0 - sigmoid_val))
    grad_pre = (cotangent.astype(jnp.float32) * slope).astype(jnp.bfloat16)
    partial_sum = lax.psum_scatter(
        lax.dot_general(
            grad_pre, aggregated, (((0,), (0,)), ((), ())), preferred_element_type=jnp.float32
        ),
        "grp",
        scatter_dimension=0,
        tiled=True,
    )
    return lax.psum_scatter(partial_sum, "rep", scatter_dimension=1, tiled=True)


def solution(mesh):
    placed = (
        P(("grp", "rep"), None),
        P("grp", "rep"),
        P("grp", "rep"),
        P(("grp", "rep"), None),
        P(("grp", "rep"), None),
        P(("grp", "rep"), None, None, None),
        P(),
        P(),
        P(),
        P(("grp", "rep"), None),
    )
    body = fused if (mesh.shape["grp"], mesh.shape["rep"]) == (4, 8) else plain
    return jax.shard_map(
        body, mesh=mesh, in_specs=placed, out_specs=P("grp", "rep"), check_vma=False
    )
```

```python
import functools

import jax
import jax.numpy as jnp
from jax import lax
from jax.experimental import pallas as pl
from jax.experimental.pallas import tpu as pltpu
from jax.sharding import PartitionSpec as P

MESH = pl.DeviceIdType.MESH
BF16 = jnp.bfloat16
F32 = jnp.float32


def dot(a, b, ca=1, cb=0):
    return lax.dot_general(a, b, (((ca,), (cb,)), ((), ())), preferred_element_type=F32)


def kernel(
    feat_hbm, row_hbm, live_hbm, seed_hbm, block_hbm, tile_hbm, self_hbm, neigh_hbm, bias_hbm, cot_hbm,
    out_ref,
    feat, row, live, seeds, block, tile, w_self, w_neigh, bias, cot,
    request, asked, table_rows, fetched, mixed, hidden, agg_t,
    send_c, recv_c, own, send_1, recv_1, send_2, recv_2, send_3, recv_3,
    load_sem, ask_send, ask_recv, row_send, row_recv,
    c_send, c_recv, s1_send, s1_recv, s2_send, s2_recv, s3_send, s3_recv,
):
    g, r = lax.axis_index("grp"), lax.axis_index("rep")
    x, c = g // 2, g % 2
    z, y = r // 2, r % 2
    n_z = recv_3.shape[0] + 1
    slots = row.shape[1]
    lanes, part = own.shape[-1], own.shape[-2]
    n_f, width_f = fetched.shape[0], fetched.shape[3]
    sib, x_near, x_far = x * 2 + (1 - c), (1 - x) * 2 + c, (1 - x) * 2 + (1 - c)
    group = (x_near, x_far, sib)
    y_near = z * 2 + (1 - y)

    def at(grp, rep):
        return {"grp": grp, "rep": rep}

    barrier = pltpu.get_barrier_semaphore()
    for peer in group:
        pl.semaphore_signal(barrier, inc=1, device_id=at(peer, r), device_id_type=MESH)
    pl.semaphore_signal(barrier, inc=1, device_id=at(g, y_near), device_id_type=MESH)
    pl.semaphore_signal(barrier, inc=1, device_id=at(sib, y_near), device_id_type=MESH)
    for d in range(1, n_z):
        pl.semaphore_signal(barrier, inc=1, device_id=at(g, (z + d) % n_z * 2 + y), device_id_type=MESH)

    loads = {}

    def load(name, src, dst):
        copy = pltpu.make_async_copy(src, dst, load_sem.at[sum(len(v) for v in loads.values())])
        copy.start()
        loads.setdefault(name, []).append(copy)

    def ready(*names):
        for name in names:
            for copy in loads[name]:
                copy.wait()

    hidden_order = (x_far, sib, x_near, g)

    def load_hidden(name, src, dst):
        for k, unit in enumerate(hidden_order):
            cols = pl.ds(pl.multiple_of(unit * lanes, lanes), lanes)
            load(name, src.at[:, cols], dst.at[:, k * lanes : (k + 1) * lanes])

    load("ask", row_hbm, row)
    load("ask", live_hbm, live)
    load("feat", feat_hbm, feat)

    ready("ask")
    slot_ix = lax.broadcasted_iota(jnp.int32, (1, slots), 1)
    for p in range(4):
        line = jnp.where(slot_ix < live[0:1, p : p + 1], row[p : p + 1, :], -1)
        line = jnp.broadcast_to(line, (8, slots))
        request[p, :, 0:slots] = line
        request[p, :, slots : 2 * slots] = line
    pl.semaphore_wait(barrier, 4 + n_z)

    asks = []
    for k, peer in enumerate(group):
        copy = pltpu.make_async_remote_copy(
            src_ref=request.at[peer], dst_ref=asked.at[g], send_sem=ask_send.at[k], recv_sem=ask_recv.at[k],
            device_id=at(peer, r), device_id_type=MESH,
        )
        copy.start()
        asks.append(copy)
    asked[g] = request[g]
    load("seeds", seed_hbm, seeds)
    load_hidden("self", self_hbm, w_self)
    load("tile", block_hbm, block)
    load("tile", tile_hbm, tile)
    load_hidden("bias", bias_hbm, bias)
    load_hidden("neigh", neigh_hbm, w_neigh)
    load_hidden("cot", cot_hbm, cot)
    ready("feat")

    def picks(chip):
        lane = lax.broadcasted_iota(jnp.int32, (1, 2 * slots), 1)
        ix = jnp.where(lane < slots, asked[2 * chip][0:1, :], asked[2 * chip + 1][0:1, :])
        rows_ix = lax.broadcasted_iota(jnp.int32, (feat.shape[0], 2 * slots), 0)
        return jnp.where(rows_ix == ix, 1.0, 0.0).astype(BF16).T

    def gather(pick, chip, f):
        rows = dot(pick, feat[:, f * width_f : (f + 1) * width_f]).astype(BF16)
        table_rows[f, 2 * chip] = rows[0:slots]
        table_rows[f, 2 * chip + 1] = rows[slots : 2 * slots]

    rows_out = {}

    def send_rows(k, f):
        copy = pltpu.make_async_remote_copy(
            src_ref=table_rows.at[f, group[k]], dst_ref=fetched.at[f, g], send_sem=row_send.at[f, k],
            recv_sem=row_recv.at[f, k], device_id=at(group[k], r), device_id_type=MESH,
        )
        copy.start()
        rows_out[f, k] = copy

    asks[0].wait_recv()
    asks[1].wait_recv()
    pick = picks(1 - x)
    for f in range(n_f):
        gather(pick, 1 - x, f)
        send_rows(0, f)
        send_rows(1, f)
    asks[2].wait_recv()
    pick = picks(x)
    for f in range(n_f):
        gather(pick, x, f)
        send_rows(2, f)
        fetched[f, g] = table_rows[f, g]

    ready("seeds", "self")
    hidden[...] = dot(seeds[...], w_self[...])
    ready("tile")
    n_b, n_k, rows_b, cols_b = tile.shape
    order = block[...]
    for b in range(n_b):
        for j in range(n_k):
            total = jnp.zeros((rows_b, cols_b), F32)
            for k in range(n_k):
                here = jnp.broadcast_to(order[k : k + 1, b : b + 1], (rows_b, cols_b)) == j
                total = jnp.where(here, tile[b, k].astype(F32), total)
            mixed[b * rows_b : (b + 1) * rows_b, j * cols_b : (j + 1) * cols_b] = total.astype(BF16)
    ready("bias", "neigh", "cot")
    hidden[...] += bias[...]

    for f in range(n_f):
        for k in range(3):
            rows_out[f, k].wait_recv()
        cols = slice(f * width_f, (f + 1) * width_f)
        agg = dot(mixed[...], fetched[f].reshape(4 * slots, width_f)).astype(BF16)
        if f < n_f - 1:
            hidden[...] += dot(agg, w_neigh[cols, :])
        agg_t[cols, :] = agg.T

    def grad(side):
        units = slice(side * 2 * lanes, (side + 1) * 2 * lanes)
        pre = hidden[:, units] + dot(agg, w_neigh[cols, units])
        sig = 0.5 * jnp.tanh(0.5 * pre) + 0.5
        return (cot[:, units].astype(F32) * (sig * (1.0 + pre * (1.0 - sig)))).astype(BF16)

    offsets = ((2, 1), (3, 0))

    def weight_part(grad_side, q, ref, kind):
        lhs = []
        for d in offsets[q]:
            for rep_y in (1 - y, y):
                first = pl.multiple_of(((z + d) % n_z * 2 + rep_y) * 2 * part, 2 * part)
                lhs.append(agg_t[pl.ds(first, 2 * part), :])
        value = dot(jnp.concatenate(lhs, axis=0), grad_side)
        for dd in range(2):
            for ry in range(2):
                for h in range(2):
                    lo = ((dd * 2 + ry) * 2 + h) * part
                    for rx in range(2):
                        piece = value[lo : lo + part, rx * lanes : (rx + 1) * lanes].astype(kind)
                        first, second = (rx, ry) if h == 0 else (ry, rx)
                        if ref is own and q == 0 and first == 0:
                            send_1[q, h, second, dd] = piece.astype(BF16)
                        else:
                            ref[q, h, first, second, dd] = piece

    def exchange(src, dst, sends, recvs, peer):
        copy = pltpu.make_async_remote_copy(
            src_ref=src, dst_ref=dst, send_sem=sends, recv_sem=recvs, device_id=peer, device_id_type=MESH
        )
        copy.start()
        return copy

    near = (at(x_near, r), at(g, y_near))
    far = (at(x_far, r), at(sib, y_near))
    core_out, outs_1, outs_2, outs_3 = {}, {}, {}, []

    def to_core(q, h, i, peer):
        k = (q * 2 + h) * 2 + i
        core_out[q, h, i] = exchange(send_c.at[q, h, i], recv_c.at[q, h, i], c_send.at[k], c_recv.at[k], peer)

    grad_side = grad(0)
    weight_part(grad_side, 0, send_c, BF16)
    for h in range(2):
        to_core(0, h, 0, far[h])
    weight_part(grad_side, 1, send_c, BF16)
    for h in range(2):
        to_core(1, h, 0, at(sib, r))
    for h in range(2):
        to_core(1, h, 1, at(sib, r))
        to_core(0, h, 1, at(sib, r))
    grad_side = grad(1)
    for q in range(2):
        weight_part(grad_side, q, own, F32)
        for h in range(2):
            if q == 1:
                core_out[q, h, 0].wait_recv()
                send_1[q, h] = (own[q, h, 0] + recv_c[q, h, 0].astype(F32)).astype(BF16)
            outs_1[q, h] = exchange(send_1.at[q, h], recv_1.at[q, h], s1_send.at[q, h], s1_recv.at[q, h], near[h])
    for q in range(2):
        for h in range(2):
            core_out[q, h, 1].wait_recv()
            kept = own[q, h, 1] + recv_c[q, h, 1].astype(F32)
            if q == 0:
                core_out[q, h, 0].wait_recv()
                kept = kept + recv_c[q, h, 0].astype(F32)
            outs_1[q, h].wait_recv()
            kept = kept + recv_1[q, h].astype(F32)
            send_2[q, h] = kept[0].astype(BF16)
            outs_2[q, h] = exchange(send_2.at[q, h], recv_2.at[q, h], s2_send.at[q, h], s2_recv.at[q, h], near[1 - h])
            own[q, h, 1, 1] = kept[1]
    for q in range(2):
        for h in range(2):
            outs_2[q, h].wait_recv()
            for dd, d in enumerate(offsets[q]):
                done = own[q, h, 1, 1, dd] + recv_2[q, h, dd].astype(F32)
                if d > 0:
                    send_3[d - 1, h] = done.astype(BF16)
                else:
                    own[q, h, 1, 1, dd] = done
        for d in offsets[q]:
            if d > 0:
                to = at(g, (z + d) % n_z * 2 + y)
                outs_3.append(exchange(send_3.at[d - 1], recv_3.at[d - 1], s3_send.at[d - 1], s3_recv.at[d - 1], to))
    total = jnp.concatenate([own[1, h, 1, 1, 1] for h in range(2)], axis=0)
    for copy in outs_3:
        copy.wait_recv()
    for d in range(n_z - 1):
        total = total + recv_3[d].astype(F32).reshape(total.shape)
    out_ref[...] = total
    for copies in (asks, rows_out.values(), core_out.values(), outs_1.values(), outs_2.values(), outs_3):
        for copy in copies:
            copy.wait_send()


def fused(features, fetch_row, live_count, seed_features, tile_block, tile_weight, self_weight, neighbour_weight, layer_bias, cotangent):
    width, hid = neighbour_weight.shape
    seeds = seed_features.shape[0]
    slots = fetch_row.shape[1]
    n_z, n_f = 4, 3
    lanes = hid // 4
    part = width // (4 * n_z)
    bias = layer_bias.reshape(1, hid)
    operands = (features, fetch_row, live_count.T, seed_features, tile_block.T, tile_weight, self_weight, neighbour_weight, bias, cotangent)
    n_b, n_k, rows_b, cols_b = tile_weight.shape
    vmem = pltpu.VMEM
    dma = pltpu.SemaphoreType.DMA
    result = pl.pallas_call(
        kernel,
        out_shape=vmem((width // (2 * n_z), lanes), F32),
        in_specs=[pl.BlockSpec(memory_space=pltpu.HBM)] * len(operands),
        out_specs=pl.BlockSpec(memory_space=vmem),
        scratch_shapes=[vmem(a.shape, a.dtype) for a in operands] + [
            vmem((4, 8, 2 * slots), jnp.int32),
            vmem((4, 8, 2 * slots), jnp.int32),
            vmem((n_f, 4, slots, width // n_f), BF16),
            vmem((n_f, 4, slots, width // n_f), BF16),
            vmem((seeds, n_k * cols_b), BF16),
            vmem((seeds, hid), F32),
            vmem((width, seeds), BF16),
            vmem((2, 2, 2, 2, 2, part, lanes), BF16),
            vmem((2, 2, 2, 2, 2, part, lanes), BF16),
            vmem((2, 2, 2, 2, 2, part, lanes), F32),
            vmem((2, 2, 2, 2, part, lanes), BF16),
            vmem((2, 2, 2, 2, part, lanes), BF16),
            vmem((2, 2, 2, part, lanes), BF16),
            vmem((2, 2, 2, part, lanes), BF16),
            vmem((n_z - 1, 2, part, lanes), BF16),
            vmem((n_z - 1, 2, part, lanes), BF16),
            dma((22,)), dma((3,)), dma((3,)), dma((n_f, 3)), dma((n_f, 3)),
            dma((8,)), dma((8,)), dma((2, 2)), dma((2, 2)), dma((2, 2)), dma((2, 2)), dma((n_z - 1,)), dma((n_z - 1,)),
        ],
        compiler_params=pltpu.CompilerParams(
            collective_id=0, has_side_effects=True, vmem_limit_bytes=56 * 1024 * 1024
        ),
        name="sage_step",
    )(*operands)
    return result.T


def plain(
    features,
    fetch_row,
    live_count,
    seed_features,
    tile_block,
    tile_weight,
    self_weight,
    neighbour_weight,
    layer_bias,
    cotangent,
):
    width = features.shape[1]
    asked = lax.all_to_all(fetch_row, "grp", split_axis=0, concat_axis=0, tiled=True)
    table_rows = jnp.take(features, asked.reshape(-1), axis=0).reshape(asked.shape + (width,))
    fetched = lax.all_to_all(table_rows, "grp", split_axis=0, concat_axis=0, tiled=True)
    live_mask = lax.broadcasted_iota(jnp.int32, fetch_row.shape, 1) < live_count
    fetched = jnp.where(live_mask[:, :, None], fetched, jnp.zeros((), fetched.dtype))
    row_blocks = fetched.reshape(-1, 128, width)
    chosen = jnp.take(row_blocks, tile_block, axis=0)
    aggregated = jnp.einsum(
        "bkij,bkjf->bif", tile_weight, chosen, preferred_element_type=jnp.float32
    )
    aggregated = aggregated.reshape(-1, width).astype(jnp.bfloat16)
    pre_act = jnp.dot(seed_features, self_weight, preferred_element_type=jnp.float32)
    pre_act = pre_act + jnp.dot(aggregated, neighbour_weight, preferred_element_type=jnp.float32)
    pre_act = pre_act + layer_bias[None, :]
    sigmoid_val = jax.nn.sigmoid(pre_act)
    slope = sigmoid_val * (1.0 + pre_act * (1.0 - sigmoid_val))
    grad_pre = (cotangent.astype(jnp.float32) * slope).astype(jnp.bfloat16)
    partial_sum = lax.psum_scatter(
        lax.dot_general(
            grad_pre, aggregated, (((0,), (0,)), ((), ())), preferred_element_type=jnp.float32
        ),
        "grp",
        scatter_dimension=0,
        tiled=True,
    )
    return lax.psum_scatter(partial_sum, "rep", scatter_dimension=1, tiled=True)


def solution(mesh):
    placed = (
        P(("grp", "rep"), None),
        P("grp", "rep"),
        P("grp", "rep"),
        P(("grp", "rep"), None),
        P(("grp", "rep"), None),
        P(("grp", "rep"), None, None, None),
        P(),
        P(),
        P(),
        P(("grp", "rep"), None),
    )
    body = fused if (mesh.shape["grp"], mesh.shape["rep"]) == (4, 8) else plain
    return jax.shard_map(
        body, mesh=mesh, in_specs=placed, out_specs=P("grp", "rep"), check_vma=False
    )
```

```python
import functools

import jax
import jax.numpy as jnp
from jax import lax
from jax.experimental import pallas as pl
from jax.experimental.pallas import tpu as pltpu
from jax.sharding import PartitionSpec as P

MESH = pl.DeviceIdType.MESH
BF16 = jnp.bfloat16
F32 = jnp.float32
CHUNKS = ((0, 2), (2, 4))
DIRECT = (0,)


def dot(a, b, ca=1, cb=0):
    return lax.dot_general(a, b, (((ca,), (cb,)), ((), ())), preferred_element_type=F32)


def kernel(
    feat_hbm, row_hbm, live_hbm, seed_hbm, block_hbm, tile_hbm, self_hbm, neigh_hbm, bias_hbm, cot_hbm,
    out_ref,
    feat, row, live, seeds, block, tile, w_self, w_neigh, bias, cot,
    request, asked, table_rows, fetched, mixed, hidden, agg_t,
    send_c, recv_c, own, send_1, recv_1, send_2, recv_2, send_3, recv_3,
    load_sem, ask_send, ask_recv, row_send, row_recv,
    c_send, c_recv, s1_send, s1_recv, s2_send, s2_recv, s3_send, s3_recv,
):
    g, r = lax.axis_index("grp"), lax.axis_index("rep")
    x, c = g // 2, g % 2
    z, y = r // 2, r % 2
    n_z = recv_3.shape[0] + 1
    slots = row.shape[1]
    lanes, part = own.shape[-1], own.shape[-2]
    n_f, width_f = fetched.shape[0], fetched.shape[3]
    sib, x_near, x_far = x * 2 + (1 - c), (1 - x) * 2 + c, (1 - x) * 2 + (1 - c)
    group = (x_near, x_far, sib)
    y_near = z * 2 + (1 - y)

    def at(grp, rep):
        return {"grp": grp, "rep": rep}

    barrier = pltpu.get_barrier_semaphore()
    for peer in group:
        pl.semaphore_signal(barrier, inc=1, device_id=at(peer, r), device_id_type=MESH)
    pl.semaphore_signal(barrier, inc=1, device_id=at(g, y_near), device_id_type=MESH)
    pl.semaphore_signal(barrier, inc=1, device_id=at(sib, y_near), device_id_type=MESH)
    for d in range(1, n_z):
        pl.semaphore_signal(barrier, inc=1, device_id=at(g, (z + d) % n_z * 2 + y), device_id_type=MESH)

    loads = {}

    def load(name, src, dst):
        copy = pltpu.make_async_copy(src, dst, load_sem.at[sum(len(v) for v in loads.values())])
        copy.start()
        loads.setdefault(name, []).append(copy)

    def ready(*names):
        for name in names:
            for copy in loads[name]:
                copy.wait()

    hidden_order = (x_far, sib, x_near, g)

    def load_hidden(name, src, dst):
        for k, unit in enumerate(hidden_order):
            cols = pl.ds(pl.multiple_of(unit * lanes, lanes), lanes)
            load(name, src.at[:, cols], dst.at[:, k * lanes : (k + 1) * lanes])

    load("ask", row_hbm, row)
    load("ask", live_hbm, live)
    load("feat", feat_hbm, feat)

    ready("ask")
    slot_ix = lax.broadcasted_iota(jnp.int32, (1, slots), 1)
    for p in range(4):
        line = jnp.where(slot_ix < live[0:1, p : p + 1], row[p : p + 1, :], -1)
        line = jnp.broadcast_to(line, (8, slots))
        request[p, :, 0:slots] = line
        request[p, :, slots : 2 * slots] = line
    pl.semaphore_wait(barrier, 4 + n_z)

    asks = []
    for k, peer in enumerate(group):
        copy = pltpu.make_async_remote_copy(
            src_ref=request.at[peer], dst_ref=asked.at[g], send_sem=ask_send.at[k], recv_sem=ask_recv.at[k],
            device_id=at(peer, r), device_id_type=MESH,
        )
        copy.start()
        asks.append(copy)
    asked[g] = request[g]
    load("seeds", seed_hbm, seeds)
    load_hidden("self", self_hbm, w_self)
    load("tile", block_hbm, block)
    load("tile", tile_hbm, tile)
    load_hidden("bias", bias_hbm, bias)
    load_hidden("neigh", neigh_hbm, w_neigh)
    load_hidden("cot", cot_hbm, cot)
    ready("feat")

    def picks(chip):
        lane = lax.broadcasted_iota(jnp.int32, (1, 2 * slots), 1)
        ix = jnp.where(lane < slots, asked[2 * chip][0:1, :], asked[2 * chip + 1][0:1, :])
        rows_ix = lax.broadcasted_iota(jnp.int32, (feat.shape[0], 2 * slots), 0)
        return jnp.where(rows_ix == ix, 1.0, 0.0).astype(BF16).T

    def gather(pick, chip, f):
        rows = dot(pick, feat[:, f * width_f : (f + 1) * width_f]).astype(BF16)
        table_rows[f, 2 * chip] = rows[0:slots]
        table_rows[f, 2 * chip + 1] = rows[slots : 2 * slots]

    rows_out = {}

    def send_rows(k, f):
        copy = pltpu.make_async_remote_copy(
            src_ref=table_rows.at[f, group[k]], dst_ref=fetched.at[f, g], send_sem=row_send.at[f, k],
            recv_sem=row_recv.at[f, k], device_id=at(group[k], r), device_id_type=MESH,
        )
        copy.start()
        rows_out[f, k] = copy

    asks[0].wait_recv()
    asks[1].wait_recv()
    pick = picks(1 - x)
    for f in range(n_f):
        gather(pick, 1 - x, f)
        send_rows(0, f)
        send_rows(1, f)
    asks[2].wait_recv()
    pick = picks(x)
    for f in range(n_f):
        gather(pick, x, f)
        send_rows(2, f)
        fetched[f, g] = table_rows[f, g]

    ready("seeds", "self")
    hidden[...] = dot(seeds[...], w_self[...])
    ready("tile")
    n_b, n_k, rows_b, cols_b = tile.shape
    order = block[...]
    for b in range(n_b):
        for j in range(n_k):
            total = jnp.zeros((rows_b, cols_b), F32)
            for k in range(n_k):
                here = jnp.broadcast_to(order[k : k + 1, b : b + 1], (rows_b, cols_b)) == j
                total = jnp.where(here, tile[b, k].astype(F32), total)
            mixed[b * rows_b : (b + 1) * rows_b, j * cols_b : (j + 1) * cols_b] = total.astype(BF16)
    ready("bias", "neigh", "cot")
    hidden[...] += bias[...]

    for f in range(n_f):
        for k in range(3):
            rows_out[f, k].wait_recv()
        cols = slice(f * width_f, (f + 1) * width_f)
        agg = dot(mixed[...], fetched[f].reshape(4 * slots, width_f)).astype(BF16)
        if f < n_f - 1:
            hidden[...] += dot(agg, w_neigh[cols, :])
        agg_t[cols, :] = agg.T

    def grad(side):
        units = slice(side * 2 * lanes, (side + 1) * 2 * lanes)
        pre = hidden[:, units] + dot(agg, w_neigh[cols, units])
        sig = 0.5 * jnp.tanh(0.5 * pre) + 0.5
        return (cot[:, units].astype(F32) * (sig * (1.0 + pre * (1.0 - sig)))).astype(BF16)

    def z_by(m):
        return (z, z + 1 - 2 * (z % 2), (z + 2) % n_z, n_z - 1 - z)[m]

    z_order = tuple(range(n_z - 1, -1, -1))
    bounds = CHUNKS

    def weight_part(grad_side, q, ref, kind):
        lhs = []
        for m in z_order[slice(*bounds[q])]:
            for rep_y in (1 - y, y):
                first = pl.multiple_of((z_by(m) * 2 + rep_y) * 2 * part, 2 * part)
                lhs.append(agg_t[pl.ds(first, 2 * part), :])
        value = dot(jnp.concatenate(lhs, axis=0), grad_side)
        for k in range(bounds[q][1] - bounds[q][0]):
            at_z = bounds[q][0] + k
            for ry in range(2):
                for h in range(2):
                    lo = ((k * 2 + ry) * 2 + h) * part
                    for rx in range(2):
                        piece = value[lo : lo + part, rx * lanes : (rx + 1) * lanes].astype(kind)
                        first, second = (rx, ry) if h == 0 else (ry, rx)
                        if ref is own and q in DIRECT and first == 0:
                            send_1[h, second, at_z] = piece.astype(BF16)
                        else:
                            ref[h, first, second, at_z] = piece

    def exchange(src, dst, sends, recvs, peer):
        copy = pltpu.make_async_remote_copy(
            src_ref=src, dst_ref=dst, send_sem=sends, recv_sem=recvs, device_id=peer, device_id_type=MESH
        )
        copy.start()
        return copy

    near = (at(x_near, r), at(g, y_near))
    far = (at(x_far, r), at(sib, y_near))
    core_out, outs_1, outs_2, outs_3 = {}, {}, {}, []

    def to_core(q, h, i, peer):
        sl = pl.ds(bounds[q][0], bounds[q][1] - bounds[q][0])
        k = (q * 2 + h) * 2 + i
        core_out[q, h, i] = exchange(send_c.at[h, i, :, sl], recv_c.at[h, i, :, sl], c_send.at[k], c_recv.at[k], peer)

    chunks = range(len(bounds))
    grad_side = grad(0)
    for q in chunks:
        weight_part(grad_side, q, send_c, BF16)
        for i in range(2):
            for h in range(2):
                to_core(q, h, i, far[h] if q in DIRECT and i == 0 else at(sib, r))
    grad_side = grad(1)
    for q in chunks:
        weight_part(grad_side, q, own, F32)
        zs = slice(*bounds[q])
        sl = pl.ds(bounds[q][0], bounds[q][1] - bounds[q][0])
        for h in range(2):
            if q not in DIRECT:
                core_out[q, h, 0].wait_recv()
                send_1[h, :, zs] = (own[h, 0, :, zs] + recv_c[h, 0, :, zs].astype(F32)).astype(BF16)
            k = q * 2 + h
            outs_1[q, h] = exchange(send_1.at[h, :, sl], recv_1.at[h, :, sl], s1_send.at[k], s1_recv.at[k], near[h])
    for q in chunks:
        zs = slice(*bounds[q])
        sl = pl.ds(bounds[q][0], bounds[q][1] - bounds[q][0])
        for h in range(2):
            core_out[q, h, 1].wait_recv()
            kept = own[h, 1, :, zs] + recv_c[h, 1, :, zs].astype(F32)
            if q in DIRECT:
                core_out[q, h, 0].wait_recv()
                kept = kept + recv_c[h, 0, :, zs].astype(F32)
            outs_1[q, h].wait_recv()
            kept = kept + recv_1[h, :, zs].astype(F32)
            send_2[h, zs] = kept[0].astype(BF16)
            k = q * 2 + h
            outs_2[q, h] = exchange(send_2.at[h, sl], recv_2.at[h, sl], s2_send.at[k], s2_recv.at[k], near[1 - h])
            own[h, 1, 1, zs] = kept[1]
    for q in chunks:
        for h in range(2):
            outs_2[q, h].wait_recv()
            for at_z in range(*bounds[q]):
                done = own[h, 1, 1, at_z] + recv_2[h, at_z].astype(F32)
                if z_order[at_z] > 0:
                    send_3[z_order[at_z] - 1, h] = done.astype(BF16)
                else:
                    own[h, 1, 1, at_z] = done
        for m in z_order[slice(*bounds[q])]:
            if m > 0:
                to = at(g, z_by(m) * 2 + y)
                outs_3.append(exchange(send_3.at[m - 1], recv_3.at[m - 1], s3_send.at[m - 1], s3_recv.at[m - 1], to))
    total = jnp.concatenate([own[h, 1, 1, n_z - 1] for h in range(2)], axis=0)
    for copy in outs_3:
        copy.wait_recv()
    for d in range(n_z - 1):
        total = total + recv_3[d].astype(F32).reshape(total.shape)
    out_ref[...] = total
    for copies in (asks, rows_out.values(), core_out.values(), outs_1.values(), outs_2.values(), outs_3):
        for copy in copies:
            copy.wait_send()


def fused(features, fetch_row, live_count, seed_features, tile_block, tile_weight, self_weight, neighbour_weight, layer_bias, cotangent):
    width, hid = neighbour_weight.shape
    seeds = seed_features.shape[0]
    slots = fetch_row.shape[1]
    n_z, n_f = 4, 3
    lanes = hid // 4
    part = width // (4 * n_z)
    bias = layer_bias.reshape(1, hid)
    operands = (features, fetch_row, live_count.T, seed_features, tile_block.T, tile_weight, self_weight, neighbour_weight, bias, cotangent)
    n_b, n_k, rows_b, cols_b = tile_weight.shape
    vmem = pltpu.VMEM
    dma = pltpu.SemaphoreType.DMA
    result = pl.pallas_call(
        kernel,
        out_shape=vmem((width // (2 * n_z), lanes), F32),
        in_specs=[pl.BlockSpec(memory_space=pltpu.HBM)] * len(operands),
        out_specs=pl.BlockSpec(memory_space=vmem),
        scratch_shapes=[vmem(a.shape, a.dtype) for a in operands] + [
            vmem((4, 8, 2 * slots), jnp.int32),
            vmem((4, 8, 2 * slots), jnp.int32),
            vmem((n_f, 4, slots, width // n_f), BF16),
            vmem((n_f, 4, slots, width // n_f), BF16),
            vmem((seeds, n_k * cols_b), BF16),
            vmem((seeds, hid), F32),
            vmem((width, seeds), BF16),
            vmem((2, 2, 2, n_z, part, lanes), BF16),
            vmem((2, 2, 2, n_z, part, lanes), BF16),
            vmem((2, 2, 2, n_z, part, lanes), F32),
            vmem((2, 2, n_z, part, lanes), BF16),
            vmem((2, 2, n_z, part, lanes), BF16),
            vmem((2, n_z, part, lanes), BF16),
            vmem((2, n_z, part, lanes), BF16),
            vmem((n_z - 1, 2, part, lanes), BF16),
            vmem((n_z - 1, 2, part, lanes), BF16),
            dma((22,)), dma((3,)), dma((3,)), dma((n_f, 3)), dma((n_f, 3)),
            *[dma((4 * len(CHUNKS),))] * 2, *[dma((2 * len(CHUNKS),))] * 4, dma((n_z - 1,)), dma((n_z - 1,)),
        ],
        compiler_params=pltpu.CompilerParams(
            collective_id=0, has_side_effects=True, vmem_limit_bytes=56 * 1024 * 1024
        ),
        name="sage_step",
    )(*operands)
    return result.T


def plain(
    features,
    fetch_row,
    live_count,
    seed_features,
    tile_block,
    tile_weight,
    self_weight,
    neighbour_weight,
    layer_bias,
    cotangent,
):
    width = features.shape[1]
    asked = lax.all_to_all(fetch_row, "grp", split_axis=0, concat_axis=0, tiled=True)
    table_rows = jnp.take(features, asked.reshape(-1), axis=0).reshape(asked.shape + (width,))
    fetched = lax.all_to_all(table_rows, "grp", split_axis=0, concat_axis=0, tiled=True)
    live_mask = lax.broadcasted_iota(jnp.int32, fetch_row.shape, 1) < live_count
    fetched = jnp.where(live_mask[:, :, None], fetched, jnp.zeros((), fetched.dtype))
    row_blocks = fetched.reshape(-1, 128, width)
    chosen = jnp.take(row_blocks, tile_block, axis=0)
    aggregated = jnp.einsum(
        "bkij,bkjf->bif", tile_weight, chosen, preferred_element_type=jnp.float32
    )
    aggregated = aggregated.reshape(-1, width).astype(jnp.bfloat16)
    pre_act = jnp.dot(seed_features, self_weight, preferred_element_type=jnp.float32)
    pre_act = pre_act + jnp.dot(aggregated, neighbour_weight, preferred_element_type=jnp.float32)
    pre_act = pre_act + layer_bias[None, :]
    sigmoid_val = jax.nn.sigmoid(pre_act)
    slope = sigmoid_val * (1.0 + pre_act * (1.0 - sigmoid_val))
    grad_pre = (cotangent.astype(jnp.float32) * slope).astype(jnp.bfloat16)
    partial_sum = lax.psum_scatter(
        lax.dot_general(
            grad_pre, aggregated, (((0,), (0,)), ((), ())), preferred_element_type=jnp.float32
        ),
        "grp",
        scatter_dimension=0,
        tiled=True,
    )
    return lax.psum_scatter(partial_sum, "rep", scatter_dimension=1, tiled=True)


def solution(mesh):
    placed = (
        P(("grp", "rep"), None),
        P("grp", "rep"),
        P("grp", "rep"),
        P(("grp", "rep"), None),
        P(("grp", "rep"), None),
        P(("grp", "rep"), None, None, None),
        P(),
        P(),
        P(),
        P(("grp", "rep"), None),
    )
    body = fused if (mesh.shape["grp"], mesh.shape["rep"]) == (4, 8) else plain
    return jax.shard_map(
        body, mesh=mesh, in_specs=placed, out_specs=P("grp", "rep"), check_vma=False
    )
```

```python
import functools

import jax
import jax.numpy as jnp
from jax import lax
from jax.experimental import pallas as pl
from jax.experimental.pallas import tpu as pltpu
from jax.sharding import PartitionSpec as P

MESH = pl.DeviceIdType.MESH
BF16 = jnp.bfloat16
F32 = jnp.float32
CHUNKS = ((0, 2), (2, 4))
DIRECT = (0,)


def dot(a, b, ca=1, cb=0):
    return lax.dot_general(a, b, (((ca,), (cb,)), ((), ())), preferred_element_type=F32)


def kernel(
    feat_hbm, row_hbm, live_hbm, seed_hbm, block_hbm, tile_hbm, self_hbm, neigh_hbm, bias_hbm, cot_hbm,
    out_ref,
    feat, row, live, seeds, block, tile, w_self, w_neigh, bias, cot,
    request, asked, table_rows, fetched, mixed, hidden, agg_t,
    send_c, recv_c, own, send_1, recv_1, send_2, recv_2, send_3, recv_3,
    load_sem, ask_send, ask_recv, row_send, row_recv,
    c_send, c_recv, s1_send, s1_recv, s2_send, s2_recv, s3_send, s3_recv,
):
    g, r = lax.axis_index("grp"), lax.axis_index("rep")
    x, c = g // 2, g % 2
    z, y = r // 2, r % 2
    n_z = recv_3.shape[0] + 1
    slots = row.shape[1]
    lanes, part = own.shape[-1], own.shape[-2]
    n_f, width_f = fetched.shape[0], fetched.shape[3]
    sib, x_near, x_far = x * 2 + (1 - c), (1 - x) * 2 + c, (1 - x) * 2 + (1 - c)
    group = (x_near, x_far, sib)
    y_near = z * 2 + (1 - y)

    def at(grp, rep):
        return {"grp": grp, "rep": rep}

    barrier = pltpu.get_barrier_semaphore()
    for peer in group:
        pl.semaphore_signal(barrier, inc=1, device_id=at(peer, r), device_id_type=MESH)
    pl.semaphore_signal(barrier, inc=1, device_id=at(g, y_near), device_id_type=MESH)
    pl.semaphore_signal(barrier, inc=1, device_id=at(sib, y_near), device_id_type=MESH)
    for d in range(1, n_z):
        pl.semaphore_signal(barrier, inc=1, device_id=at(g, (z + d) % n_z * 2 + y), device_id_type=MESH)

    loads = {}

    def load(name, src, dst):
        copy = pltpu.make_async_copy(src, dst, load_sem.at[sum(len(v) for v in loads.values())])
        copy.start()
        loads.setdefault(name, []).append(copy)

    def ready(*names):
        for name in names:
            for copy in loads[name]:
                copy.wait()

    hidden_order = (x_far, sib, x_near, g)

    def load_hidden(name, src, dst):
        for k, unit in enumerate(hidden_order):
            cols = pl.ds(pl.multiple_of(unit * lanes, lanes), lanes)
            load(name, src.at[:, cols], dst.at[:, k * lanes : (k + 1) * lanes])

    load("ask", row_hbm, row)
    load("ask", live_hbm, live)
    load("feat", feat_hbm, feat)

    ready("ask")
    slot_ix = lax.broadcasted_iota(jnp.int32, (1, slots), 1)
    for p in range(4):
        line = jnp.where(slot_ix < live[0:1, p : p + 1], row[p : p + 1, :], -1)
        line = jnp.broadcast_to(line, (8, slots))
        request[p, :, 0:slots] = line
        request[p, :, slots : 2 * slots] = line
    pl.semaphore_wait(barrier, 4 + n_z)

    asks = []
    for k, peer in enumerate(group):
        copy = pltpu.make_async_remote_copy(
            src_ref=request.at[peer], dst_ref=asked.at[g], send_sem=ask_send.at[k], recv_sem=ask_recv.at[k],
            device_id=at(peer, r), device_id_type=MESH,
        )
        copy.start()
        asks.append(copy)
    asked[g] = request[g]
    load("seeds", seed_hbm, seeds)
    load_hidden("self", self_hbm, w_self)
    load("tile", block_hbm, block)
    load("tile", tile_hbm, tile)
    load_hidden("bias", bias_hbm, bias)
    load_hidden("neigh", neigh_hbm, w_neigh)
    load_hidden("cot", cot_hbm, cot)
    ready("feat")

    def picks(chip):
        lane = lax.broadcasted_iota(jnp.int32, (1, 2 * slots), 1)
        ix = jnp.where(lane < slots, asked[2 * chip][0:1, :], asked[2 * chip + 1][0:1, :])
        column = jnp.broadcast_to(ix, (2 * slots, 2 * slots)).T
        column = jnp.concatenate([column] * (feat.shape[0] // (2 * slots)), axis=1)
        rows_ix = lax.broadcasted_iota(jnp.int32, (2 * slots, feat.shape[0]), 1)
        return jnp.where(rows_ix == column, 1.0, 0.0).astype(BF16)

    def gather(pick, chip, f):
        rows = dot(pick, feat[:, f * width_f : (f + 1) * width_f]).astype(BF16)
        table_rows[f, 2 * chip] = rows[0:slots]
        table_rows[f, 2 * chip + 1] = rows[slots : 2 * slots]

    rows_out = {}

    def send_rows(k, f):
        copy = pltpu.make_async_remote_copy(
            src_ref=table_rows.at[f, group[k]], dst_ref=fetched.at[f, g], send_sem=row_send.at[f, k],
            recv_sem=row_recv.at[f, k], device_id=at(group[k], r), device_id_type=MESH,
        )
        copy.start()
        rows_out[f, k] = copy

    asks[0].wait_recv()
    asks[1].wait_recv()
    pick = picks(1 - x)
    for f in range(n_f):
        gather(pick, 1 - x, f)
        send_rows(0, f)
        send_rows(1, f)
    asks[2].wait_recv()
    pick = picks(x)
    for f in range(n_f):
        gather(pick, x, f)
        send_rows(2, f)
        fetched[f, g] = table_rows[f, g]

    ready("seeds", "self")
    hidden[...] = dot(seeds[...], w_self[...])
    ready("tile")
    n_b, n_k, rows_b, cols_b = tile.shape
    order = block[...]
    for b in range(n_b):
        for j in range(n_k):
            total = jnp.zeros((rows_b, cols_b), F32)
            for k in range(n_k):
                here = jnp.broadcast_to(order[k : k + 1, b : b + 1], (rows_b, cols_b)) == j
                total = jnp.where(here, tile[b, k].astype(F32), total)
            mixed[b * rows_b : (b + 1) * rows_b, j * cols_b : (j + 1) * cols_b] = total.astype(BF16)
    ready("bias", "neigh", "cot")
    hidden[...] += bias[...]

    for f in range(n_f):
        for k in range(3):
            rows_out[f, k].wait_recv()
        cols = slice(f * width_f, (f + 1) * width_f)
        agg = dot(mixed[...], fetched[f].reshape(4 * slots, width_f)).astype(BF16)
        if f < n_f - 1:
            hidden[...] += dot(agg, w_neigh[cols, :])
        agg_t[cols, :] = agg.T

    def grad(side):
        units = slice(side * 2 * lanes, (side + 1) * 2 * lanes)
        pre = hidden[:, units] + dot(agg, w_neigh[cols, units])
        sig = 0.5 * jnp.tanh(0.5 * pre) + 0.5
        return (cot[:, units].astype(F32) * (sig * (1.0 + pre * (1.0 - sig)))).astype(BF16)

    def z_by(m):
        return (z, z + 1 - 2 * (z % 2), (z + 2) % n_z, n_z - 1 - z)[m]

    z_order = tuple(range(n_z - 1, -1, -1))
    bounds = CHUNKS

    def weight_part(grad_side, q, ref, kind):
        lhs = []
        for m in z_order[slice(*bounds[q])]:
            for rep_y in (1 - y, y):
                first = pl.multiple_of((z_by(m) * 2 + rep_y) * 2 * part, 2 * part)
                lhs.append(agg_t[pl.ds(first, 2 * part), :])
        value = dot(jnp.concatenate(lhs, axis=0), grad_side)
        for k in range(bounds[q][1] - bounds[q][0]):
            at_z = bounds[q][0] + k
            for ry in range(2):
                for h in range(2):
                    lo = ((k * 2 + ry) * 2 + h) * part
                    for rx in range(2):
                        piece = value[lo : lo + part, rx * lanes : (rx + 1) * lanes].astype(kind)
                        first, second = (rx, ry) if h == 0 else (ry, rx)
                        if ref is own and q in DIRECT and first == 0:
                            send_1[h, second, at_z] = piece.astype(BF16)
                        else:
                            ref[h, first, second, at_z] = piece

    def exchange(src, dst, sends, recvs, peer):
        copy = pltpu.make_async_remote_copy(
            src_ref=src, dst_ref=dst, send_sem=sends, recv_sem=recvs, device_id=peer, device_id_type=MESH
        )
        copy.start()
        return copy

    near = (at(x_near, r), at(g, y_near))
    far = (at(x_far, r), at(sib, y_near))
    core_out, outs_1, outs_2, outs_3 = {}, {}, {}, []

    def to_core(q, k, peer, *part_of):
        place = part_of + (pl.ds(bounds[q][0], bounds[q][1] - bounds[q][0]),)
        k = q * 3 + k
        return exchange(send_c.at[place], recv_c.at[place], c_send.at[k], c_recv.at[k], peer)

    every = slice(None)
    chunks = range(len(bounds))
    grad_side = grad(0)
    for q in chunks:
        weight_part(grad_side, q, send_c, BF16)
        if q in DIRECT:
            core_out[q] = [to_core(q, h, far[h], h, 0, every) for h in range(2)]
            core_out[q].append(to_core(q, 2, at(sib, r), every, 1, every))
        else:
            core_out[q] = [to_core(q, 0, at(sib, r), every, every, every)]
    grad_side = grad(1)
    for q in chunks:
        weight_part(grad_side, q, own, F32)
        zs = slice(*bounds[q])
        sl = pl.ds(bounds[q][0], bounds[q][1] - bounds[q][0])
        if q not in DIRECT:
            core_out[q][0].wait_recv()
        for h in range(2):
            if q not in DIRECT:
                send_1[h, :, zs] = (own[h, 0, :, zs] + recv_c[h, 0, :, zs].astype(F32)).astype(BF16)
            k = q * 2 + h
            outs_1[q, h] = exchange(send_1.at[h, :, sl], recv_1.at[h, :, sl], s1_send.at[k], s1_recv.at[k], near[h])
    for q in chunks:
        zs = slice(*bounds[q])
        sl = pl.ds(bounds[q][0], bounds[q][1] - bounds[q][0])
        for h in range(2):
            if q in DIRECT and h == 0:
                core_out[q][2].wait_recv()
            kept = own[h, 1, :, zs] + recv_c[h, 1, :, zs].astype(F32)
            if q in DIRECT:
                core_out[q][h].wait_recv()
                kept = kept + recv_c[h, 0, :, zs].astype(F32)
            outs_1[q, h].wait_recv()
            kept = kept + recv_1[h, :, zs].astype(F32)
            send_2[h, zs] = kept[0].astype(BF16)
            k = q * 2 + h
            outs_2[q, h] = exchange(send_2.at[h, sl], recv_2.at[h, sl], s2_send.at[k], s2_recv.at[k], near[1 - h])
            own[h, 1, 1, zs] = kept[1]
    for q in chunks:
        for h in range(2):
            outs_2[q, h].wait_recv()
            for at_z in range(*bounds[q]):
                done = own[h, 1, 1, at_z] + recv_2[h, at_z].astype(F32)
                if z_order[at_z] > 0:
                    send_3[z_order[at_z] - 1, h] = done.astype(BF16)
                else:
                    own[h, 1, 1, at_z] = done
        for m in z_order[slice(*bounds[q])]:
            if m > 0:
                to = at(g, z_by(m) * 2 + y)
                outs_3.append(exchange(send_3.at[m - 1], recv_3.at[m - 1], s3_send.at[m - 1], s3_recv.at[m - 1], to))
    total = jnp.concatenate([own[h, 1, 1, n_z - 1] for h in range(2)], axis=0)
    for copy in outs_3:
        copy.wait_recv()
    for d in range(n_z - 1):
        total = total + recv_3[d].astype(F32).reshape(total.shape)
    out_ref[...] = total
    for copies in (asks, rows_out.values(), *core_out.values(), outs_1.values(), outs_2.values(), outs_3):
        for copy in copies:
            copy.wait_send()


def fused(features, fetch_row, live_count, seed_features, tile_block, tile_weight, self_weight, neighbour_weight, layer_bias, cotangent):
    width, hid = neighbour_weight.shape
    seeds = seed_features.shape[0]
    slots = fetch_row.shape[1]
    n_z, n_f = 4, 3
    lanes = hid // 4
    part = width // (4 * n_z)
    bias = layer_bias.reshape(1, hid)
    operands = (features, fetch_row, live_count.T, seed_features, tile_block.T, tile_weight, self_weight, neighbour_weight, bias, cotangent)
    n_b, n_k, rows_b, cols_b = tile_weight.shape
    vmem = pltpu.VMEM
    dma = pltpu.SemaphoreType.DMA
    result = pl.pallas_call(
        kernel,
        out_shape=vmem((width // (2 * n_z), lanes), F32),
        in_specs=[pl.BlockSpec(memory_space=pltpu.HBM)] * len(operands),
        out_specs=pl.BlockSpec(memory_space=vmem),
        scratch_shapes=[vmem(a.shape, a.dtype) for a in operands] + [
            vmem((4, 8, 2 * slots), jnp.int32),
            vmem((4, 8, 2 * slots), jnp.int32),
            vmem((n_f, 4, slots, width // n_f), BF16),
            vmem((n_f, 4, slots, width // n_f), BF16),
            vmem((seeds, n_k * cols_b), BF16),
            vmem((seeds, hid), F32),
            vmem((width, seeds), BF16),
            vmem((2, 2, 2, n_z, part, lanes), BF16),
            vmem((2, 2, 2, n_z, part, lanes), BF16),
            vmem((2, 2, 2, n_z, part, lanes), F32),
            vmem((2, 2, n_z, part, lanes), BF16),
            vmem((2, 2, n_z, part, lanes), BF16),
            vmem((2, n_z, part, lanes), BF16),
            vmem((2, n_z, part, lanes), BF16),
            vmem((n_z - 1, 2, part, lanes), BF16),
            vmem((n_z - 1, 2, part, lanes), BF16),
            dma((22,)), dma((3,)), dma((3,)), dma((n_f, 3)), dma((n_f, 3)),
            *[dma((3 * len(CHUNKS),))] * 2, *[dma((2 * len(CHUNKS),))] * 4, dma((n_z - 1,)), dma((n_z - 1,)),
        ],
        compiler_params=pltpu.CompilerParams(
            collective_id=0, has_side_effects=True, vmem_limit_bytes=56 * 1024 * 1024
        ),
        name="sage_step",
    )(*operands)
    return result.T


def plain(
    features,
    fetch_row,
    live_count,
    seed_features,
    tile_block,
    tile_weight,
    self_weight,
    neighbour_weight,
    layer_bias,
    cotangent,
):
    width = features.shape[1]
    asked = lax.all_to_all(fetch_row, "grp", split_axis=0, concat_axis=0, tiled=True)
    table_rows = jnp.take(features, asked.reshape(-1), axis=0).reshape(asked.shape + (width,))
    fetched = lax.all_to_all(table_rows, "grp", split_axis=0, concat_axis=0, tiled=True)
    live_mask = lax.broadcasted_iota(jnp.int32, fetch_row.shape, 1) < live_count
    fetched = jnp.where(live_mask[:, :, None], fetched, jnp.zeros((), fetched.dtype))
    row_blocks = fetched.reshape(-1, 128, width)
    chosen = jnp.take(row_blocks, tile_block, axis=0)
    aggregated = jnp.einsum(
        "bkij,bkjf->bif", tile_weight, chosen, preferred_element_type=jnp.float32
    )
    aggregated = aggregated.reshape(-1, width).astype(jnp.bfloat16)
    pre_act = jnp.dot(seed_features, self_weight, preferred_element_type=jnp.float32)
    pre_act = pre_act + jnp.dot(aggregated, neighbour_weight, preferred_element_type=jnp.float32)
    pre_act = pre_act + layer_bias[None, :]
    sigmoid_val = jax.nn.sigmoid(pre_act)
    slope = sigmoid_val * (1.0 + pre_act * (1.0 - sigmoid_val))
    grad_pre = (cotangent.astype(jnp.float32) * slope).astype(jnp.bfloat16)
    partial_sum = lax.psum_scatter(
        lax.dot_general(
            grad_pre, aggregated, (((0,), (0,)), ((), ())), preferred_element_type=jnp.float32
        ),
        "grp",
        scatter_dimension=0,
        tiled=True,
    )
    return lax.psum_scatter(partial_sum, "rep", scatter_dimension=1, tiled=True)


def solution(mesh):
    placed = (
        P(("grp", "rep"), None),
        P("grp", "rep"),
        P("grp", "rep"),
        P(("grp", "rep"), None),
        P(("grp", "rep"), None),
        P(("grp", "rep"), None, None, None),
        P(),
        P(),
        P(),
        P(("grp", "rep"), None),
    )
    body = fused if (mesh.shape["grp"], mesh.shape["rep"]) == (4, 8) else plain
    return jax.shard_map(
        body, mesh=mesh, in_specs=placed, out_specs=P("grp", "rep"), check_vma=False
    )
```

```python
import functools

import jax
import jax.numpy as jnp
from jax import lax
from jax.experimental import pallas as pl
from jax.experimental.pallas import tpu as pltpu
from jax.sharding import PartitionSpec as P

MESH = pl.DeviceIdType.MESH
BF16 = jnp.bfloat16
F32 = jnp.float32
CHUNKS = ((0, 1), (1, 2), (2, 4))
DIRECT = (0, 1)


def dot(a, b, ca=1, cb=0):
    return lax.dot_general(a, b, (((ca,), (cb,)), ((), ())), preferred_element_type=F32)


def kernel(
    feat_hbm, row_hbm, live_hbm, seed_hbm, block_hbm, tile_hbm, self_hbm, neigh_hbm, bias_hbm, cot_hbm,
    out_ref,
    feat, row, live, seeds, block, tile, w_self, w_neigh, bias, cot,
    request, asked, table_rows, fetched, mixed, hidden, agg_t,
    send_c, recv_c, own, send_1, recv_1, send_2, recv_2, send_3, recv_3, send_m, recv_m,
    load_sem, ask_send, ask_recv, row_send, row_recv,
    c_send, c_recv, s1_send, s1_recv, s2_send, s2_recv, s3_send, s3_recv, m_send, m_recv,
):
    g, r = lax.axis_index("grp"), lax.axis_index("rep")
    x, c = g // 2, g % 2
    z, y = r // 2, r % 2
    n_z = recv_3.shape[0] + 1
    slots = row.shape[1]
    lanes, part = own.shape[-1], own.shape[-2]
    n_f, width_f = fetched.shape[0], fetched.shape[3]
    sib, x_near, x_far = x * 2 + (1 - c), (1 - x) * 2 + c, (1 - x) * 2 + (1 - c)
    group = (x_near, x_far, sib)
    y_near = z * 2 + (1 - y)

    def at(grp, rep):
        return {"grp": grp, "rep": rep}

    barrier = pltpu.get_barrier_semaphore()
    for peer in group:
        pl.semaphore_signal(barrier, inc=1, device_id=at(peer, r), device_id_type=MESH)
    pl.semaphore_signal(barrier, inc=1, device_id=at(g, y_near), device_id_type=MESH)
    pl.semaphore_signal(barrier, inc=1, device_id=at(sib, y_near), device_id_type=MESH)
    for d in range(1, n_z):
        pl.semaphore_signal(barrier, inc=1, device_id=at(g, (z + d) % n_z * 2 + y), device_id_type=MESH)
    z_next = z + 1 - 2 * (z % 2)
    pl.semaphore_signal(barrier, inc=1, device_id=at(g, z_next * 2 + 1 - y), device_id_type=MESH)
    pl.semaphore_signal(barrier, inc=1, device_id=at(x_near, z_next * 2 + y), device_id_type=MESH)

    loads = {}

    def load(name, src, dst):
        copy = pltpu.make_async_copy(src, dst, load_sem.at[sum(len(v) for v in loads.values())])
        copy.start()
        loads.setdefault(name, []).append(copy)

    def ready(*names):
        for name in names:
            for copy in loads[name]:
                copy.wait()

    hidden_order = (x_far, sib, x_near, g)

    def load_hidden(name, src, dst):
        for k, unit in enumerate(hidden_order):
            cols = pl.ds(pl.multiple_of(unit * lanes, lanes), lanes)
            load(name, src.at[:, cols], dst.at[:, k * lanes : (k + 1) * lanes])

    load("ask", row_hbm, row)
    load("ask", live_hbm, live)
    load("feat", feat_hbm, feat)

    ready("ask")
    slot_ix = lax.broadcasted_iota(jnp.int32, (1, slots), 1)
    for p in range(4):
        line = jnp.where(slot_ix < live[0:1, p : p + 1], row[p : p + 1, :], -1)
        line = jnp.broadcast_to(line, (8, slots))
        request[p, :, 0:slots] = line
        request[p, :, slots : 2 * slots] = line
    pl.semaphore_wait(barrier, 6 + n_z)

    asks = []
    for k, peer in enumerate(group):
        copy = pltpu.make_async_remote_copy(
            src_ref=request.at[peer], dst_ref=asked.at[g], send_sem=ask_send.at[k], recv_sem=ask_recv.at[k],
            device_id=at(peer, r), device_id_type=MESH,
        )
        copy.start()
        asks.append(copy)
    asked[g] = request[g]
    load("seeds", seed_hbm, seeds)
    load_hidden("self", self_hbm, w_self)
    load("tile", block_hbm, block)
    load("tile", tile_hbm, tile)
    load_hidden("bias", bias_hbm, bias)
    load_hidden("neigh", neigh_hbm, w_neigh)
    load_hidden("cot", cot_hbm, cot)
    ready("feat")

    def picks(chip):
        lane = lax.broadcasted_iota(jnp.int32, (1, 2 * slots), 1)
        ix = jnp.where(lane < slots, asked[2 * chip][0:1, :], asked[2 * chip + 1][0:1, :])
        column = jnp.broadcast_to(ix, (2 * slots, 2 * slots)).T
        column = jnp.concatenate([column] * (feat.shape[0] // (2 * slots)), axis=1)
        rows_ix = lax.broadcasted_iota(jnp.int32, (2 * slots, feat.shape[0]), 1)
        return jnp.where(rows_ix == column, 1.0, 0.0).astype(BF16)

    def gather(pick, chip, f):
        rows = dot(pick, feat[:, f * width_f : (f + 1) * width_f]).astype(BF16)
        table_rows[f, 2 * chip] = rows[0:slots]
        table_rows[f, 2 * chip + 1] = rows[slots : 2 * slots]

    rows_out = {}

    def send_rows(k, f):
        copy = pltpu.make_async_remote_copy(
            src_ref=table_rows.at[f, group[k]], dst_ref=fetched.at[f, g], send_sem=row_send.at[f, k],
            recv_sem=row_recv.at[f, k], device_id=at(group[k], r), device_id_type=MESH,
        )
        copy.start()
        rows_out[f, k] = copy

    asks[0].wait_recv()
    asks[1].wait_recv()
    pick = picks(1 - x)
    for f in range(n_f):
        gather(pick, 1 - x, f)
        send_rows(0, f)
        send_rows(1, f)
    asks[2].wait_recv()
    pick = picks(x)
    for f in range(n_f):
        gather(pick, x, f)
        send_rows(2, f)
        fetched[f, g] = table_rows[f, g]

    ready("seeds", "self")
    hidden[...] = dot(seeds[...], w_self[...])
    ready("tile")
    n_b, n_k, rows_b, cols_b = tile.shape
    order = block[...]
    for b in range(n_b):
        for j in range(n_k):
            total = jnp.zeros((rows_b, cols_b), F32)
            for k in range(n_k):
                here = jnp.broadcast_to(order[k : k + 1, b : b + 1], (rows_b, cols_b)) == j
                total = jnp.where(here, tile[b, k].astype(F32), total)
            mixed[b * rows_b : (b + 1) * rows_b, j * cols_b : (j + 1) * cols_b] = total.astype(BF16)
    ready("bias", "neigh", "cot")
    hidden[...] += bias[...]

    for f in range(n_f):
        for k in range(3):
            rows_out[f, k].wait_recv()
        cols = slice(f * width_f, (f + 1) * width_f)
        agg = dot(mixed[...], fetched[f].reshape(4 * slots, width_f)).astype(BF16)
        if f < n_f - 1:
            hidden[...] += dot(agg, w_neigh[cols, :])
        agg_t[cols, :] = agg.T

    def grad(side):
        units = slice(side * 2 * lanes, (side + 1) * 2 * lanes)
        pre = hidden[:, units] + dot(agg, w_neigh[cols, units])
        sig = 0.5 * jnp.tanh(0.5 * pre) + 0.5
        return (cot[:, units].astype(F32) * (sig * (1.0 + pre * (1.0 - sig)))).astype(BF16)

    def z_by(m):
        return (z, z + 1 - 2 * (z % 2), (z + 2) % n_z, n_z - 1 - z)[m]

    z_order = tuple(range(n_z - 1, -1, -1))
    bounds = CHUNKS

    def weight_part(grad_side, q, ref, kind):
        lhs = []
        for m in z_order[slice(*bounds[q])]:
            for rep_y in (1 - y, y):
                first = pl.multiple_of((z_by(m) * 2 + rep_y) * 2 * part, 2 * part)
                lhs.append(agg_t[pl.ds(first, 2 * part), :])
        value = dot(jnp.concatenate(lhs, axis=0), grad_side)
        for k in range(bounds[q][1] - bounds[q][0]):
            at_z = bounds[q][0] + k
            for ry in range(2):
                for h in range(2):
                    lo = ((k * 2 + ry) * 2 + h) * part
                    for rx in range(2):
                        piece = value[lo : lo + part, rx * lanes : (rx + 1) * lanes].astype(kind)
                        first, second = (rx, ry) if h == 0 else (ry, rx)
                        if ref is own and q in DIRECT and first == 0:
                            send_1[h, second, at_z] = piece.astype(BF16)
                        else:
                            ref[h, first, second, at_z] = piece

    def exchange(src, dst, sends, recvs, peer):
        copy = pltpu.make_async_remote_copy(
            src_ref=src, dst_ref=dst, send_sem=sends, recv_sem=recvs, device_id=peer, device_id_type=MESH
        )
        copy.start()
        return copy

    near = (at(x_near, r), at(g, y_near))
    far = (at(x_far, r), at(sib, y_near))
    core_out, outs_1, outs_2, outs_3, outs_m = {}, {}, {}, [], []
    cross = (at(g, z_by(1) * 2 + 1 - y), at(x_near, z_by(1) * 2 + y))

    def to_core(q, k, peer, *part_of):
        place = part_of + (pl.ds(bounds[q][0], bounds[q][1] - bounds[q][0]),)
        k = q * 3 + k
        return exchange(send_c.at[place], recv_c.at[place], c_send.at[k], c_recv.at[k], peer)

    every = slice(None)
    chunks = range(len(bounds))
    grad_side = grad(0)
    for q in chunks:
        weight_part(grad_side, q, send_c, BF16)
        if q in DIRECT:
            core_out[q] = [to_core(q, h, far[h], h, 0, every) for h in range(2)]
            core_out[q].append(to_core(q, 2, at(sib, r), every, 1, every))
        else:
            core_out[q] = [to_core(q, 0, at(sib, r), every, every, every)]
    grad_side = grad(1)
    for q in chunks:
        weight_part(grad_side, q, own, F32)
        zs = slice(*bounds[q])
        sl = pl.ds(bounds[q][0], bounds[q][1] - bounds[q][0])
        if q not in DIRECT:
            core_out[q][0].wait_recv()
        for h in range(2):
            if q not in DIRECT:
                send_1[h, :, zs] = (own[h, 0, :, zs] + recv_c[h, 0, :, zs].astype(F32)).astype(BF16)
            k = q * 2 + h
            outs_1[q, h] = exchange(send_1.at[h, :, sl], recv_1.at[h, :, sl], s1_send.at[k], s1_recv.at[k], near[h])
    def after_first(q, h):
        zs = slice(*bounds[q])
        kept = own[h, 1, :, zs] + recv_c[h, 1, :, zs].astype(F32)
        if q in DIRECT:
            core_out[q][h].wait_recv()
            kept = kept + recv_c[h, 0, :, zs].astype(F32)
        outs_1[q, h].wait_recv()
        return kept + recv_1[h, :, zs].astype(F32)

    def second(q):
        zs = slice(*bounds[q])
        sl = pl.ds(bounds[q][0], bounds[q][1] - bounds[q][0])
        core_out[q][2].wait_recv()
        for h in range(2):
            kept = after_first(q, h)
            send_2[h, zs] = kept[0].astype(BF16)
            k = q * 2 + h
            outs_2[q, h] = exchange(send_2.at[h, sl], recv_2.at[h, sl], s2_send.at[k], s2_recv.at[k], near[1 - h])
            own[h, 1, 1, zs] = kept[1]

    def third(q):
        for h in range(2):
            outs_2[q, h].wait_recv()
            for at_z in range(*bounds[q]):
                done = own[h, 1, 1, at_z] + recv_2[h, at_z].astype(F32)
                send_3[z_order[at_z] - 1, h] = done.astype(BF16)
        for m in z_order[slice(*bounds[q])]:
            to = at(g, z_by(m) * 2 + y)
            outs_3.append(exchange(send_3.at[m - 1], recv_3.at[m - 1], s3_send.at[m - 1], s3_recv.at[m - 1], to))

    def second_and_third(q):
        for h in range(2):
            kept = after_first(q, h)
            send_m[h, 0] = kept[0, 0].astype(BF16)
            send_m[h, 1] = kept[1, 0].astype(BF16)
            send_m[h, 2] = kept[0, 1].astype(BF16)
            peers = (cross[h], at(g, z_by(1) * 2 + y), near[1 - h])
            for i in range(3):
                k = h * 3 + i
                outs_m.append(exchange(send_m.at[h, i], recv_m.at[h, i], m_send.at[k], m_recv.at[k], peers[i]))
            own[h, 1, 1, n_z - 1] = kept[1, 1]

    second(0)
    second(1)
    third(0)
    second_and_third(2)
    third(1)
    total = jnp.concatenate([own[h, 1, 1, n_z - 1] for h in range(2)], axis=0)
    for copy in outs_m:
        copy.wait_recv()
    for i in range(3):
        total = total + jnp.concatenate([recv_m[h, i].astype(F32) for h in range(2)], axis=0)
    for copy in outs_3:
        copy.wait_recv()
    for d in range(1, n_z - 1):
        total = total + recv_3[d].astype(F32).reshape(total.shape)
    out_ref[...] = total
    for copies in (asks, rows_out.values(), *core_out.values(), outs_1.values(), outs_2.values(), outs_3, outs_m):
        for copy in copies:
            copy.wait_send()


def fused(features, fetch_row, live_count, seed_features, tile_block, tile_weight, self_weight, neighbour_weight, layer_bias, cotangent):
    width, hid = neighbour_weight.shape
    seeds = seed_features.shape[0]
    slots = fetch_row.shape[1]
    n_z, n_f = 4, 3
    lanes = hid // 4
    part = width // (4 * n_z)
    bias = layer_bias.reshape(1, hid)
    operands = (features, fetch_row, live_count.T, seed_features, tile_block.T, tile_weight, self_weight, neighbour_weight, bias, cotangent)
    n_b, n_k, rows_b, cols_b = tile_weight.shape
    vmem = pltpu.VMEM
    dma = pltpu.SemaphoreType.DMA
    result = pl.pallas_call(
        kernel,
        out_shape=vmem((width // (2 * n_z), lanes), F32),
        in_specs=[pl.BlockSpec(memory_space=pltpu.HBM)] * len(operands),
        out_specs=pl.BlockSpec(memory_space=vmem),
        scratch_shapes=[vmem(a.shape, a.dtype) for a in operands] + [
            vmem((4, 8, 2 * slots), jnp.int32),
            vmem((4, 8, 2 * slots), jnp.int32),
            vmem((n_f, 4, slots, width // n_f), BF16),
            vmem((n_f, 4, slots, width // n_f), BF16),
            vmem((seeds, n_k * cols_b), BF16),
            vmem((seeds, hid), F32),
            vmem((width, seeds), BF16),
            vmem((2, 2, 2, n_z, part, lanes), BF16),
            vmem((2, 2, 2, n_z, part, lanes), BF16),
            vmem((2, 2, 2, n_z, part, lanes), F32),
            vmem((2, 2, n_z, part, lanes), BF16),
            vmem((2, 2, n_z, part, lanes), BF16),
            vmem((2, n_z, part, lanes), BF16),
            vmem((2, n_z, part, lanes), BF16),
            vmem((n_z - 1, 2, part, lanes), BF16),
            vmem((n_z - 1, 2, part, lanes), BF16),
            vmem((2, 3, part, lanes), BF16),
            vmem((2, 3, part, lanes), BF16),
            dma((22,)), dma((3,)), dma((3,)), dma((n_f, 3)), dma((n_f, 3)),
            *[dma((3 * len(CHUNKS),))] * 2, *[dma((2 * len(CHUNKS),))] * 4, dma((n_z - 1,)), dma((n_z - 1,)), dma((6,)), dma((6,)),
        ],
        compiler_params=pltpu.CompilerParams(
            collective_id=0, has_side_effects=True, vmem_limit_bytes=56 * 1024 * 1024
        ),
        name="sage_step",
    )(*operands)
    return result.T


def plain(
    features,
    fetch_row,
    live_count,
    seed_features,
    tile_block,
    tile_weight,
    self_weight,
    neighbour_weight,
    layer_bias,
    cotangent,
):
    width = features.shape[1]
    asked = lax.all_to_all(fetch_row, "grp", split_axis=0, concat_axis=0, tiled=True)
    table_rows = jnp.take(features, asked.reshape(-1), axis=0).reshape(asked.shape + (width,))
    fetched = lax.all_to_all(table_rows, "grp", split_axis=0, concat_axis=0, tiled=True)
    live_mask = lax.broadcasted_iota(jnp.int32, fetch_row.shape, 1) < live_count
    fetched = jnp.where(live_mask[:, :, None], fetched, jnp.zeros((), fetched.dtype))
    row_blocks = fetched.reshape(-1, 128, width)
    chosen = jnp.take(row_blocks, tile_block, axis=0)
    aggregated = jnp.einsum(
        "bkij,bkjf->bif", tile_weight, chosen, preferred_element_type=jnp.float32
    )
    aggregated = aggregated.reshape(-1, width).astype(jnp.bfloat16)
    pre_act = jnp.dot(seed_features, self_weight, preferred_element_type=jnp.float32)
    pre_act = pre_act + jnp.dot(aggregated, neighbour_weight, preferred_element_type=jnp.float32)
    pre_act = pre_act + layer_bias[None, :]
    sigmoid_val = jax.nn.sigmoid(pre_act)
    slope = sigmoid_val * (1.0 + pre_act * (1.0 - sigmoid_val))
    grad_pre = (cotangent.astype(jnp.float32) * slope).astype(jnp.bfloat16)
    partial_sum = lax.psum_scatter(
        lax.dot_general(
            grad_pre, aggregated, (((0,), (0,)), ((), ())), preferred_element_type=jnp.float32
        ),
        "grp",
        scatter_dimension=0,
        tiled=True,
    )
    return lax.psum_scatter(partial_sum, "rep", scatter_dimension=1, tiled=True)


def solution(mesh):
    placed = (
        P(("grp", "rep"), None),
        P("grp", "rep"),
        P("grp", "rep"),
        P(("grp", "rep"), None),
        P(("grp", "rep"), None),
        P(("grp", "rep"), None, None, None),
        P(),
        P(),
        P(),
        P(("grp", "rep"), None),
    )
    body = fused if (mesh.shape["grp"], mesh.shape["rep"]) == (4, 8) else plain
    return jax.shard_map(
        body, mesh=mesh, in_specs=placed, out_specs=P("grp", "rep"), check_vma=False
    )
```

```python
import functools

import jax
import jax.numpy as jnp
from jax import lax
from jax.experimental import pallas as pl
from jax.experimental.pallas import tpu as pltpu
from jax.sharding import PartitionSpec as P

MESH = pl.DeviceIdType.MESH
BF16 = jnp.bfloat16
F32 = jnp.float32
CHUNKS = ((0, 1), (1, 2), (2, 4))
DIRECT = (0, 1)


def dot(a, b, ca=1, cb=0):
    return lax.dot_general(a, b, (((ca,), (cb,)), ((), ())), preferred_element_type=F32)


def kernel(
    feat_hbm, row_hbm, live_hbm, seed_hbm, block_hbm, tile_hbm, self_hbm, neigh_hbm, bias_hbm, cot_hbm,
    out_ref,
    feat, row, live, seeds, block, tile, w_self, w_neigh, bias, cot,
    request, asked, table_rows, fetched, mixed, hidden, agg_t,
    send_c, recv_c, own, send_1, recv_1, send_2, recv_2, send_3, recv_3, send_m, recv_m,
    load_sem, ask_send, ask_recv, row_send, row_recv,
    c_send, c_recv, s1_send, s1_recv, s2_send, s2_recv, s3_send, s3_recv, m_send, m_recv,
):
    g, r = lax.axis_index("grp"), lax.axis_index("rep")
    x, c = g // 2, g % 2
    z, y = r // 2, r % 2
    n_z = recv_3.shape[0] + 1
    slots = row.shape[1]
    lanes, part = own.shape[-1], own.shape[-2]
    n_f, width_f = fetched.shape[0], fetched.shape[3]
    sib, x_near, x_far = x * 2 + (1 - c), (1 - x) * 2 + c, (1 - x) * 2 + (1 - c)
    group = (x_near, x_far, sib)
    y_near = z * 2 + (1 - y)

    def at(grp, rep):
        return {"grp": grp, "rep": rep}

    loads = {}

    def load(name, src, dst):
        copy = pltpu.make_async_copy(src, dst, load_sem.at[sum(len(v) for v in loads.values())])
        copy.start()
        loads.setdefault(name, []).append(copy)

    def ready(*names):
        for name in names:
            for copy in loads[name]:
                copy.wait()

    hidden_order = (x_far, sib, x_near, g)

    def load_hidden(name, src, dst):
        for k, unit in enumerate(hidden_order):
            cols = pl.ds(pl.multiple_of(unit * lanes, lanes), lanes)
            load(name, src.at[:, cols], dst.at[:, k * lanes : (k + 1) * lanes])

    load("ask", row_hbm, row)
    load("ask", live_hbm, live)

    barrier = pltpu.get_barrier_semaphore()
    for peer in group:
        pl.semaphore_signal(barrier, inc=1, device_id=at(peer, r), device_id_type=MESH)
    pl.semaphore_signal(barrier, inc=1, device_id=at(g, y_near), device_id_type=MESH)
    pl.semaphore_signal(barrier, inc=1, device_id=at(sib, y_near), device_id_type=MESH)
    for d in range(1, n_z):
        pl.semaphore_signal(barrier, inc=1, device_id=at(g, (z + d) % n_z * 2 + y), device_id_type=MESH)
    z_next = z + 1 - 2 * (z % 2)
    pl.semaphore_signal(barrier, inc=1, device_id=at(g, z_next * 2 + 1 - y), device_id_type=MESH)
    pl.semaphore_signal(barrier, inc=1, device_id=at(x_near, z_next * 2 + y), device_id_type=MESH)

    load("feat", feat_hbm, feat)

    ready("ask")
    slot_ix = lax.broadcasted_iota(jnp.int32, (1, slots), 1)
    for p in range(4):
        line = jnp.where(slot_ix < live[0:1, p : p + 1], row[p : p + 1, :], -1)
        line = jnp.broadcast_to(line, (8, slots))
        request[p, :, 0:slots] = line
        request[p, :, slots : 2 * slots] = line
    pl.semaphore_wait(barrier, 6 + n_z)

    asks = []
    for k, peer in enumerate(group):
        copy = pltpu.make_async_remote_copy(
            src_ref=request.at[peer], dst_ref=asked.at[g], send_sem=ask_send.at[k], recv_sem=ask_recv.at[k],
            device_id=at(peer, r), device_id_type=MESH,
        )
        copy.start()
        asks.append(copy)
    asked[g] = request[g]
    load("seeds", seed_hbm, seeds)
    load_hidden("self", self_hbm, w_self)
    load("tile", block_hbm, block)
    load("tile", tile_hbm, tile)
    load_hidden("bias", bias_hbm, bias)
    load_hidden("neigh", neigh_hbm, w_neigh)
    load_hidden("cot", cot_hbm, cot)
    ready("feat")

    def picks(chip):
        lane = lax.broadcasted_iota(jnp.int32, (1, 2 * slots), 1)
        ix = jnp.where(lane < slots, asked[2 * chip][0:1, :], asked[2 * chip + 1][0:1, :])
        column = jnp.broadcast_to(ix, (2 * slots, 2 * slots)).T
        column = jnp.concatenate([column] * (feat.shape[0] // (2 * slots)), axis=1)
        rows_ix = lax.broadcasted_iota(jnp.int32, (2 * slots, feat.shape[0]), 1)
        return jnp.where(rows_ix == column, 1.0, 0.0).astype(BF16)

    def gather(pick, chip, f):
        rows = dot(pick, feat[:, f * width_f : (f + 1) * width_f]).astype(BF16)
        table_rows[f, 2 * chip] = rows[0:slots]
        table_rows[f, 2 * chip + 1] = rows[slots : 2 * slots]

    rows_out = {}

    def send_rows(k, f):
        copy = pltpu.make_async_remote_copy(
            src_ref=table_rows.at[f, group[k]], dst_ref=fetched.at[f, g], send_sem=row_send.at[f, k],
            recv_sem=row_recv.at[f, k], device_id=at(group[k], r), device_id_type=MESH,
        )
        copy.start()
        rows_out[f, k] = copy

    asks[0].wait_recv()
    asks[1].wait_recv()
    pick = picks(1 - x)
    for f in range(n_f):
        gather(pick, 1 - x, f)
        send_rows(0, f)
        send_rows(1, f)
    asks[2].wait_recv()
    pick = picks(x)
    for f in range(n_f):
        gather(pick, x, f)
        send_rows(2, f)
        fetched[f, g] = table_rows[f, g]

    ready("seeds", "self")
    hidden[...] = dot(seeds[...], w_self[...])
    ready("tile")
    n_b, n_k, rows_b, cols_b = tile.shape
    order = block[...]
    for b in range(n_b):
        for j in range(n_k):
            total = jnp.zeros((rows_b, cols_b), F32)
            for k in range(n_k):
                here = jnp.broadcast_to(order[k : k + 1, b : b + 1], (rows_b, cols_b)) == j
                total = jnp.where(here, tile[b, k].astype(F32), total)
            mixed[b * rows_b : (b + 1) * rows_b, j * cols_b : (j + 1) * cols_b] = total.astype(BF16)
    ready("bias", "neigh", "cot")
    hidden[...] += bias[...]

    for f in range(n_f):
        for k in range(3):
            rows_out[f, k].wait_recv()
        cols = slice(f * width_f, (f + 1) * width_f)
        agg = dot(mixed[...], fetched[f].reshape(4 * slots, width_f)).astype(BF16)
        if f < n_f - 1:
            hidden[...] += dot(agg, w_neigh[cols, :])
        agg_t[cols, :] = agg.T

    def grad(side):
        units = slice(side * 2 * lanes, (side + 1) * 2 * lanes)
        pre = hidden[:, units] + dot(agg, w_neigh[cols, units])
        sig = 0.5 * jnp.tanh(0.5 * pre) + 0.5
        return (cot[:, units].astype(F32) * (sig * (1.0 + pre * (1.0 - sig)))).astype(BF16)

    def z_by(m):
        return (z, z + 1 - 2 * (z % 2), (z + 2) % n_z, n_z - 1 - z)[m]

    z_order = tuple(range(n_z - 1, -1, -1))
    bounds = CHUNKS

    def weight_part(grad_side, q, ref, kind):
        lhs = []
        for m in z_order[slice(*bounds[q])]:
            for rep_y in (1 - y, y):
                first = pl.multiple_of((z_by(m) * 2 + rep_y) * 2 * part, 2 * part)
                lhs.append(agg_t[pl.ds(first, 2 * part), :])
        value = dot(jnp.concatenate(lhs, axis=0), grad_side)
        for k in range(bounds[q][1] - bounds[q][0]):
            at_z = bounds[q][0] + k
            for ry in range(2):
                for h in range(2):
                    lo = ((k * 2 + ry) * 2 + h) * part
                    for rx in range(2):
                        piece = value[lo : lo + part, rx * lanes : (rx + 1) * lanes].astype(kind)
                        first, second = (rx, ry) if h == 0 else (ry, rx)
                        if ref is own and q in DIRECT and first == 0:
                            send_1[h, second, at_z] = piece.astype(BF16)
                        else:
                            ref[h, first, second, at_z] = piece

    def exchange(src, dst, sends, recvs, peer):
        copy = pltpu.make_async_remote_copy(
            src_ref=src, dst_ref=dst, send_sem=sends, recv_sem=recvs, device_id=peer, device_id_type=MESH
        )
        copy.start()
        return copy

    near = (at(x_near, r), at(g, y_near))
    far = (at(x_far, r), at(sib, y_near))
    core_out, outs_1, outs_2, outs_3, outs_m = {}, {}, {}, [], []
    cross = (at(g, z_by(1) * 2 + 1 - y), at(x_near, z_by(1) * 2 + y))

    def to_core(q, k, peer, *part_of):
        place = part_of + (pl.ds(bounds[q][0], bounds[q][1] - bounds[q][0]),)
        k = q * 3 + k
        return exchange(send_c.at[place], recv_c.at[place], c_send.at[k], c_recv.at[k], peer)

    every = slice(None)
    chunks = range(len(bounds))
    grad_side = grad(0)
    for q in chunks:
        weight_part(grad_side, q, send_c, BF16)
        if q in DIRECT:
            core_out[q] = [to_core(q, h, far[h], h, 0, every) for h in range(2)]
            core_out[q].append(to_core(q, 2, at(sib, r), every, 1, every))
        else:
            core_out[q] = [to_core(q, 0, at(sib, r), every, every, every)]
    grad_side = grad(1)
    for q in chunks:
        weight_part(grad_side, q, own, F32)
        zs = slice(*bounds[q])
        sl = pl.ds(bounds[q][0], bounds[q][1] - bounds[q][0])
        if q not in DIRECT:
            core_out[q][0].wait_recv()
        for h in range(2):
            if q not in DIRECT:
                send_1[h, :, zs] = (own[h, 0, :, zs] + recv_c[h, 0, :, zs].astype(F32)).astype(BF16)
            k = q * 2 + h
            outs_1[q, h] = exchange(send_1.at[h, :, sl], recv_1.at[h, :, sl], s1_send.at[k], s1_recv.at[k], near[h])
    def after_first(q, h):
        zs = slice(*bounds[q])
        kept = own[h, 1, :, zs] + recv_c[h, 1, :, zs].astype(F32)
        if q in DIRECT:
            core_out[q][h].wait_recv()
            kept = kept + recv_c[h, 0, :, zs].astype(F32)
        outs_1[q, h].wait_recv()
        return kept + recv_1[h, :, zs].astype(F32)

    def second(q):
        zs = slice(*bounds[q])
        sl = pl.ds(bounds[q][0], bounds[q][1] - bounds[q][0])
        core_out[q][2].wait_recv()
        for h in range(2):
            kept = after_first(q, h)
            send_2[h, zs] = kept[0].astype(BF16)
            k = q * 2 + h
            outs_2[q, h] = exchange(send_2.at[h, sl], recv_2.at[h, sl], s2_send.at[k], s2_recv.at[k], near[1 - h])
            own[h, 1, 1, zs] = kept[1]

    def third(q):
        for h in range(2):
            outs_2[q, h].wait_recv()
            for at_z in range(*bounds[q]):
                done = own[h, 1, 1, at_z] + recv_2[h, at_z].astype(F32)
                send_3[z_order[at_z] - 1, h] = done.astype(BF16)
        for m in z_order[slice(*bounds[q])]:
            to = at(g, z_by(m) * 2 + y)
            outs_3.append(exchange(send_3.at[m - 1], recv_3.at[m - 1], s3_send.at[m - 1], s3_recv.at[m - 1], to))

    def second_and_third(q):
        for h in range(2):
            kept = after_first(q, h)
            send_m[h, 0] = kept[0, 0].astype(BF16)
            send_m[h, 1] = kept[1, 0].astype(BF16)
            send_m[h, 2] = kept[0, 1].astype(BF16)
            peers = (cross[h], at(g, z_by(1) * 2 + y), near[1 - h])
            for i in range(3):
                k = h * 3 + i
                outs_m.append(exchange(send_m.at[h, i], recv_m.at[h, i], m_send.at[k], m_recv.at[k], peers[i]))
            own[h, 1, 1, n_z - 1] = kept[1, 1]

    second(0)
    second(1)
    third(0)
    second_and_third(2)
    third(1)
    for copies in (asks, rows_out.values(), *core_out.values(), outs_1.values(), outs_2.values(), outs_3, outs_m):
        for copy in copies:
            copy.wait_send()
    total = jnp.concatenate([own[h, 1, 1, n_z - 1] for h in range(2)], axis=0)
    for copy in outs_m:
        copy.wait_recv()
    for i in range(3):
        total = total + jnp.concatenate([recv_m[h, i].astype(F32) for h in range(2)], axis=0)
    for copy in outs_3:
        copy.wait_recv()
    for d in range(1, n_z - 1):
        total = total + recv_3[d].astype(F32).reshape(total.shape)
    out_ref[...] = total


def fused(features, fetch_row, live_count, seed_features, tile_block, tile_weight, self_weight, neighbour_weight, layer_bias, cotangent):
    width, hid = neighbour_weight.shape
    seeds = seed_features.shape[0]
    slots = fetch_row.shape[1]
    n_z, n_f = 4, 3
    lanes = hid // 4
    part = width // (4 * n_z)
    bias = layer_bias.reshape(1, hid)
    operands = (features, fetch_row, live_count.T, seed_features, tile_block.T, tile_weight, self_weight, neighbour_weight, bias, cotangent)
    n_b, n_k, rows_b, cols_b = tile_weight.shape
    vmem = pltpu.VMEM
    dma = pltpu.SemaphoreType.DMA
    result = pl.pallas_call(
        kernel,
        out_shape=vmem((width // (2 * n_z), lanes), F32),
        in_specs=[pl.BlockSpec(memory_space=pltpu.HBM)] * len(operands),
        out_specs=pl.BlockSpec(memory_space=vmem),
        scratch_shapes=[vmem(a.shape, a.dtype) for a in operands] + [
            vmem((4, 8, 2 * slots), jnp.int32),
            vmem((4, 8, 2 * slots), jnp.int32),
            vmem((n_f, 4, slots, width // n_f), BF16),
            vmem((n_f, 4, slots, width // n_f), BF16),
            vmem((seeds, n_k * cols_b), BF16),
            vmem((seeds, hid), F32),
            vmem((width, seeds), BF16),
            vmem((2, 2, 2, n_z, part, lanes), BF16),
            vmem((2, 2, 2, n_z, part, lanes), BF16),
            vmem((2, 2, 2, n_z, part, lanes), F32),
            vmem((2, 2, n_z, part, lanes), BF16),
            vmem((2, 2, n_z, part, lanes), BF16),
            vmem((2, n_z, part, lanes), BF16),
            vmem((2, n_z, part, lanes), BF16),
            vmem((n_z - 1, 2, part, lanes), BF16),
            vmem((n_z - 1, 2, part, lanes), BF16),
            vmem((2, 3, part, lanes), BF16),
            vmem((2, 3, part, lanes), BF16),
            dma((22,)), dma((3,)), dma((3,)), dma((n_f, 3)), dma((n_f, 3)),
            *[dma((3 * len(CHUNKS),))] * 2, *[dma((2 * len(CHUNKS),))] * 4, dma((n_z - 1,)), dma((n_z - 1,)), dma((6,)), dma((6,)),
        ],
        compiler_params=pltpu.CompilerParams(
            collective_id=0, has_side_effects=True, vmem_limit_bytes=56 * 1024 * 1024
        ),
        name="sage_step",
    )(*operands)
    return result.T


def plain(
    features,
    fetch_row,
    live_count,
    seed_features,
    tile_block,
    tile_weight,
    self_weight,
    neighbour_weight,
    layer_bias,
    cotangent,
):
    width = features.shape[1]
    asked = lax.all_to_all(fetch_row, "grp", split_axis=0, concat_axis=0, tiled=True)
    table_rows = jnp.take(features, asked.reshape(-1), axis=0).reshape(asked.shape + (width,))
    fetched = lax.all_to_all(table_rows, "grp", split_axis=0, concat_axis=0, tiled=True)
    live_mask = lax.broadcasted_iota(jnp.int32, fetch_row.shape, 1) < live_count
    fetched = jnp.where(live_mask[:, :, None], fetched, jnp.zeros((), fetched.dtype))
    row_blocks = fetched.reshape(-1, 128, width)
    chosen = jnp.take(row_blocks, tile_block, axis=0)
    aggregated = jnp.einsum(
        "bkij,bkjf->bif", tile_weight, chosen, preferred_element_type=jnp.float32
    )
    aggregated = aggregated.reshape(-1, width).astype(jnp.bfloat16)
    pre_act = jnp.dot(seed_features, self_weight, preferred_element_type=jnp.float32)
    pre_act = pre_act + jnp.dot(aggregated, neighbour_weight, preferred_element_type=jnp.float32)
    pre_act = pre_act + layer_bias[None, :]
    sigmoid_val = jax.nn.sigmoid(pre_act)
    slope = sigmoid_val * (1.0 + pre_act * (1.0 - sigmoid_val))
    grad_pre = (cotangent.astype(jnp.float32) * slope).astype(jnp.bfloat16)
    partial_sum = lax.psum_scatter(
        lax.dot_general(
            grad_pre, aggregated, (((0,), (0,)), ((), ())), preferred_element_type=jnp.float32
        ),
        "grp",
        scatter_dimension=0,
        tiled=True,
    )
    return lax.psum_scatter(partial_sum, "rep", scatter_dimension=1, tiled=True)


def solution(mesh):
    placed = (
        P(("grp", "rep"), None),
        P("grp", "rep"),
        P("grp", "rep"),
        P(("grp", "rep"), None),
        P(("grp", "rep"), None),
        P(("grp", "rep"), None, None, None),
        P(),
        P(),
        P(),
        P(("grp", "rep"), None),
    )
    body = fused if (mesh.shape["grp"], mesh.shape["rep"]) == (4, 8) else plain
    return jax.shard_map(
        body, mesh=mesh, in_specs=placed, out_specs=P("grp", "rep"), check_vma=False
    )
```

```python
import functools

import jax
import jax.numpy as jnp
from jax import lax
from jax.experimental import pallas as pl
from jax.experimental.pallas import tpu as pltpu
from jax.sharding import PartitionSpec as P

MESH = pl.DeviceIdType.MESH
BF16 = jnp.bfloat16
F32 = jnp.float32
CHUNKS = ((0, 1), (1, 2), (2, 4))
DIRECT = (0,)


def dot(a, b, ca=1, cb=0):
    return lax.dot_general(a, b, (((ca,), (cb,)), ((), ())), preferred_element_type=F32)


def kernel(
    feat_hbm, row_hbm, live_hbm, seed_hbm, block_hbm, tile_hbm, self_hbm, neigh_hbm, bias_hbm, cot_hbm,
    out_ref,
    feat, row, live, seeds, block, tile, w_self, w_neigh, bias, cot,
    request, asked, table_rows, fetched, mixed, hidden, agg_t,
    send_c, recv_c, own, send_1, recv_1, send_2, recv_2, send_3, recv_3, send_m, recv_m,
    load_sem, ask_send, ask_recv, row_send, row_recv,
    c_send, c_recv, s1_send, s1_recv, s2_send, s2_recv, s3_send, s3_recv, m_send, m_recv,
):
    g, r = lax.axis_index("grp"), lax.axis_index("rep")
    x, c = g // 2, g % 2
    z, y = r // 2, r % 2
    n_z = recv_3.shape[0] + 1
    slots = row.shape[1]
    lanes, part = own.shape[-1], own.shape[-2]
    n_f, width_f = fetched.shape[0], fetched.shape[3]
    sib, x_near, x_far = x * 2 + (1 - c), (1 - x) * 2 + c, (1 - x) * 2 + (1 - c)
    group = (x_near, x_far, sib)
    y_near = z * 2 + (1 - y)

    def at(grp, rep):
        return {"grp": grp, "rep": rep}

    loads = {}

    def load(name, src, dst):
        copy = pltpu.make_async_copy(src, dst, load_sem.at[sum(len(v) for v in loads.values())])
        copy.start()
        loads.setdefault(name, []).append(copy)

    def ready(*names):
        for name in names:
            for copy in loads[name]:
                copy.wait()

    hidden_order = (x_far, sib, x_near, g)

    def load_hidden(name, src, dst):
        for k, unit in enumerate(hidden_order):
            cols = pl.ds(pl.multiple_of(unit * lanes, lanes), lanes)
            load(name, src.at[:, cols], dst.at[:, k * lanes : (k + 1) * lanes])

    load("ask", row_hbm, row)
    load("ask", live_hbm, live)

    barrier = pltpu.get_barrier_semaphore()
    for peer in group:
        pl.semaphore_signal(barrier, inc=1, device_id=at(peer, r), device_id_type=MESH)
    pl.semaphore_signal(barrier, inc=1, device_id=at(g, y_near), device_id_type=MESH)
    pl.semaphore_signal(barrier, inc=1, device_id=at(sib, y_near), device_id_type=MESH)
    for d in range(1, n_z):
        pl.semaphore_signal(barrier, inc=1, device_id=at(g, (z + d) % n_z * 2 + y), device_id_type=MESH)
    z_next = z + 1 - 2 * (z % 2)
    pl.semaphore_signal(barrier, inc=1, device_id=at(g, z_next * 2 + 1 - y), device_id_type=MESH)
    pl.semaphore_signal(barrier, inc=1, device_id=at(x_near, z_next * 2 + y), device_id_type=MESH)

    load("feat", feat_hbm, feat)

    ready("ask")
    slot_ix = lax.broadcasted_iota(jnp.int32, (1, slots), 1)
    for p in range(4):
        line = jnp.where(slot_ix < live[0:1, p : p + 1], row[p : p + 1, :], -1)
        line = jnp.broadcast_to(line, (8, slots))
        request[p, :, 0:slots] = line
        request[p, :, slots : 2 * slots] = line
    pl.semaphore_wait(barrier, 6 + n_z)

    asks = []
    for k, peer in enumerate(group):
        copy = pltpu.make_async_remote_copy(
            src_ref=request.at[peer], dst_ref=asked.at[g], send_sem=ask_send.at[k], recv_sem=ask_recv.at[k],
            device_id=at(peer, r), device_id_type=MESH,
        )
        copy.start()
        asks.append(copy)
    asked[g] = request[g]
    load("seeds", seed_hbm, seeds)
    load_hidden("self", self_hbm, w_self)
    load("tile", block_hbm, block)
    load("tile", tile_hbm, tile)
    load_hidden("bias", bias_hbm, bias)
    load_hidden("neigh", neigh_hbm, w_neigh)
    load_hidden("cot", cot_hbm, cot)
    ready("feat")

    def picks(chip):
        lane = lax.broadcasted_iota(jnp.int32, (1, 2 * slots), 1)
        ix = jnp.where(lane < slots, asked[2 * chip][0:1, :], asked[2 * chip + 1][0:1, :])
        column = jnp.broadcast_to(ix, (2 * slots, 2 * slots)).T
        column = jnp.concatenate([column] * (feat.shape[0] // (2 * slots)), axis=1)
        rows_ix = lax.broadcasted_iota(jnp.int32, (2 * slots, feat.shape[0]), 1)
        return jnp.where(rows_ix == column, 1.0, 0.0).astype(BF16)

    def gather(pick, chip, f):
        rows = dot(pick, feat[:, f * width_f : (f + 1) * width_f]).astype(BF16)
        table_rows[f, 2 * chip] = rows[0:slots]
        table_rows[f, 2 * chip + 1] = rows[slots : 2 * slots]

    rows_out = {}

    def send_rows(k, f):
        copy = pltpu.make_async_remote_copy(
            src_ref=table_rows.at[f, group[k]], dst_ref=fetched.at[f, g], send_sem=row_send.at[f, k],
            recv_sem=row_recv.at[f, k], device_id=at(group[k], r), device_id_type=MESH,
        )
        copy.start()
        rows_out[f, k] = copy

    asks[0].wait_recv()
    asks[1].wait_recv()
    pick = picks(1 - x)
    for f in range(n_f):
        gather(pick, 1 - x, f)
        send_rows(0, f)
        send_rows(1, f)
    asks[2].wait_recv()
    pick = picks(x)
    for f in range(n_f):
        gather(pick, x, f)
        send_rows(2, f)
        fetched[f, g] = table_rows[f, g]

    ready("seeds", "self")
    hidden[...] = dot(seeds[...], w_self[...])
    ready("tile")
    n_b, n_k, rows_b, cols_b = tile.shape
    order = block[...]
    for b in range(n_b):
        for j in range(n_k):
            total = jnp.zeros((rows_b, cols_b), F32)
            for k in range(n_k):
                here = jnp.broadcast_to(order[k : k + 1, b : b + 1], (rows_b, cols_b)) == j
                total = jnp.where(here, tile[b, k].astype(F32), total)
            mixed[b * rows_b : (b + 1) * rows_b, j * cols_b : (j + 1) * cols_b] = total.astype(BF16)
    ready("bias", "neigh", "cot")
    hidden[...] += bias[...]

    for f in range(n_f):
        for k in range(3):
            rows_out[f, k].wait_recv()
        cols = slice(f * width_f, (f + 1) * width_f)
        agg = dot(mixed[...], fetched[f].reshape(4 * slots, width_f)).astype(BF16)
        if f < n_f - 1:
            hidden[...] += dot(agg, w_neigh[cols, :])
        agg_t[cols, :] = agg.T

    def grad(side):
        units = slice(side * 2 * lanes, (side + 1) * 2 * lanes)
        pre = hidden[:, units] + dot(agg, w_neigh[cols, units])
        sig = 0.5 * jnp.tanh(0.5 * pre) + 0.5
        return (cot[:, units].astype(F32) * (sig * (1.0 + pre * (1.0 - sig)))).astype(BF16)

    def z_by(m):
        return (z, z + 1 - 2 * (z % 2), (z + 2) % n_z, n_z - 1 - z)[m]

    z_order = tuple(range(n_z - 1, -1, -1))
    bounds = CHUNKS

    def weight_part(grad_side, q, ref, kind):
        lhs = []
        for m in z_order[slice(*bounds[q])]:
            for rep_y in (1 - y, y):
                first = pl.multiple_of((z_by(m) * 2 + rep_y) * 2 * part, 2 * part)
                lhs.append(agg_t[pl.ds(first, 2 * part), :])
        value = dot(jnp.concatenate(lhs, axis=0), grad_side)
        for k in range(bounds[q][1] - bounds[q][0]):
            at_z = bounds[q][0] + k
            for ry in range(2):
                for h in range(2):
                    lo = ((k * 2 + ry) * 2 + h) * part
                    for rx in range(2):
                        piece = value[lo : lo + part, rx * lanes : (rx + 1) * lanes].astype(kind)
                        first, second = (rx, ry) if h == 0 else (ry, rx)
                        if ref is own and q in DIRECT and first == 0:
                            send_1[h, second, at_z] = piece.astype(BF16)
                        else:
                            ref[h, first, second, at_z] = piece

    def exchange(src, dst, sends, recvs, peer):
        copy = pltpu.make_async_remote_copy(
            src_ref=src, dst_ref=dst, send_sem=sends, recv_sem=recvs, device_id=peer, device_id_type=MESH
        )
        copy.start()
        return copy

    near = (at(x_near, r), at(g, y_near))
    far = (at(x_far, r), at(sib, y_near))
    core_out, outs_1, outs_2, outs_3, outs_m = {}, {}, {}, [], []
    cross = (at(g, z_by(1) * 2 + 1 - y), at(x_near, z_by(1) * 2 + y))

    def to_core(q, k, peer, *part_of):
        place = part_of + (pl.ds(bounds[q][0], bounds[q][1] - bounds[q][0]),)
        k = q * 3 + k
        return exchange(send_c.at[place], recv_c.at[place], c_send.at[k], c_recv.at[k], peer)

    every = slice(None)
    chunks = range(len(bounds))
    grad_side = grad(0)
    for q in chunks:
        weight_part(grad_side, q, send_c, BF16)
        if q in DIRECT:
            core_out[q] = [to_core(q, h, far[h], h, 0, every) for h in range(2)]
            core_out[q].append(to_core(q, 2, at(sib, r), every, 1, every))
        else:
            core_out[q] = [to_core(q, 0, at(sib, r), every, every, every)]
    grad_side = grad(1)
    for q in chunks:
        weight_part(grad_side, q, own, F32)
        zs = slice(*bounds[q])
        sl = pl.ds(bounds[q][0], bounds[q][1] - bounds[q][0])
        if q not in DIRECT:
            core_out[q][0].wait_recv()
        for h in range(2):
            if q not in DIRECT:
                send_1[h, :, zs] = (own[h, 0, :, zs] + recv_c[h, 0, :, zs].astype(F32)).astype(BF16)
            k = q * 2 + h
            outs_1[q, h] = exchange(send_1.at[h, :, sl], recv_1.at[h, :, sl], s1_send.at[k], s1_recv.at[k], near[h])
    def after_first(q, h):
        zs = slice(*bounds[q])
        kept = own[h, 1, :, zs] + recv_c[h, 1, :, zs].astype(F32)
        if q in DIRECT:
            core_out[q][h].wait_recv()
            kept = kept + recv_c[h, 0, :, zs].astype(F32)
        outs_1[q, h].wait_recv()
        return kept + recv_1[h, :, zs].astype(F32)

    def second(q):
        zs = slice(*bounds[q])
        sl = pl.ds(bounds[q][0], bounds[q][1] - bounds[q][0])
        if q in DIRECT:
            core_out[q][2].wait_recv()
        for h in range(2):
            kept = after_first(q, h)
            send_2[h, zs] = kept[0].astype(BF16)
            k = q * 2 + h
            outs_2[q, h] = exchange(send_2.at[h, sl], recv_2.at[h, sl], s2_send.at[k], s2_recv.at[k], near[1 - h])
            own[h, 1, 1, zs] = kept[1]

    def third(q):
        for h in range(2):
            outs_2[q, h].wait_recv()
            for at_z in range(*bounds[q]):
                done = own[h, 1, 1, at_z] + recv_2[h, at_z].astype(F32)
                send_3[z_order[at_z] - 1, h] = done.astype(BF16)
        for m in z_order[slice(*bounds[q])]:
            to = at(g, z_by(m) * 2 + y)
            outs_3.append(exchange(send_3.at[m - 1], recv_3.at[m - 1], s3_send.at[m - 1], s3_recv.at[m - 1], to))

    def second_and_third(q):
        for h in range(2):
            kept = after_first(q, h)
            send_m[h, 0] = kept[0, 0].astype(BF16)
            send_m[h, 1] = kept[1, 0].astype(BF16)
            send_m[h, 2] = kept[0, 1].astype(BF16)
            peers = (cross[h], at(g, z_by(1) * 2 + y), near[1 - h])
            for i in range(3):
                k = h * 3 + i
                outs_m.append(exchange(send_m.at[h, i], recv_m.at[h, i], m_send.at[k], m_recv.at[k], peers[i]))
            own[h, 1, 1, n_z - 1] = kept[1, 1]

    second(0)
    second(1)
    third(0)
    second_and_third(2)
    third(1)
    for copies in (asks, rows_out.values(), *core_out.values(), outs_1.values(), outs_2.values(), outs_3, outs_m):
        for copy in copies:
            copy.wait_send()
    total = jnp.concatenate([own[h, 1, 1, n_z - 1] for h in range(2)], axis=0)
    for copy in outs_m:
        copy.wait_recv()
    for i in range(3):
        total = total + jnp.concatenate([recv_m[h, i].astype(F32) for h in range(2)], axis=0)
    for copy in outs_3:
        copy.wait_recv()
    for d in range(1, n_z - 1):
        total = total + recv_3[d].astype(F32).reshape(total.shape)
    out_ref[...] = total


def fused(features, fetch_row, live_count, seed_features, tile_block, tile_weight, self_weight, neighbour_weight, layer_bias, cotangent):
    width, hid = neighbour_weight.shape
    seeds = seed_features.shape[0]
    slots = fetch_row.shape[1]
    n_z, n_f = 4, 3
    lanes = hid // 4
    part = width // (4 * n_z)
    bias = layer_bias.reshape(1, hid)
    operands = (features, fetch_row, live_count.T, seed_features, tile_block.T, tile_weight, self_weight, neighbour_weight, bias, cotangent)
    n_b, n_k, rows_b, cols_b = tile_weight.shape
    vmem = pltpu.VMEM
    dma = pltpu.SemaphoreType.DMA
    result = pl.pallas_call(
        kernel,
        out_shape=vmem((width // (2 * n_z), lanes), F32),
        in_specs=[pl.BlockSpec(memory_space=pltpu.HBM)] * len(operands),
        out_specs=pl.BlockSpec(memory_space=vmem),
        scratch_shapes=[vmem(a.shape, a.dtype) for a in operands] + [
            vmem((4, 8, 2 * slots), jnp.int32),
            vmem((4, 8, 2 * slots), jnp.int32),
            vmem((n_f, 4, slots, width // n_f), BF16),
            vmem((n_f, 4, slots, width // n_f), BF16),
            vmem((seeds, n_k * cols_b), BF16),
            vmem((seeds, hid), F32),
            vmem((width, seeds), BF16),
            vmem((2, 2, 2, n_z, part, lanes), BF16),
            vmem((2, 2, 2, n_z, part, lanes), BF16),
            vmem((2, 2, 2, n_z, part, lanes), F32),
            vmem((2, 2, n_z, part, lanes), BF16),
            vmem((2, 2, n_z, part, lanes), BF16),
            vmem((2, n_z, part, lanes), BF16),
            vmem((2, n_z, part, lanes), BF16),
            vmem((n_z - 1, 2, part, lanes), BF16),
            vmem((n_z - 1, 2, part, lanes), BF16),
            vmem((2, 3, part, lanes), BF16),
            vmem((2, 3, part, lanes), BF16),
            dma((22,)), dma((3,)), dma((3,)), dma((n_f, 3)), dma((n_f, 3)),
            *[dma((3 * len(CHUNKS),))] * 2, *[dma((2 * len(CHUNKS),))] * 4, dma((n_z - 1,)), dma((n_z - 1,)), dma((6,)), dma((6,)),
        ],
        compiler_params=pltpu.CompilerParams(
            collective_id=0, has_side_effects=True, vmem_limit_bytes=56 * 1024 * 1024
        ),
        name="sage_step",
    )(*operands)
    return result.T


def plain(
    features,
    fetch_row,
    live_count,
    seed_features,
    tile_block,
    tile_weight,
    self_weight,
    neighbour_weight,
    layer_bias,
    cotangent,
):
    width = features.shape[1]
    asked = lax.all_to_all(fetch_row, "grp", split_axis=0, concat_axis=0, tiled=True)
    table_rows = jnp.take(features, asked.reshape(-1), axis=0).reshape(asked.shape + (width,))
    fetched = lax.all_to_all(table_rows, "grp", split_axis=0, concat_axis=0, tiled=True)
    live_mask = lax.broadcasted_iota(jnp.int32, fetch_row.shape, 1) < live_count
    fetched = jnp.where(live_mask[:, :, None], fetched, jnp.zeros((), fetched.dtype))
    row_blocks = fetched.reshape(-1, 128, width)
    chosen = jnp.take(row_blocks, tile_block, axis=0)
    aggregated = jnp.einsum(
        "bkij,bkjf->bif", tile_weight, chosen, preferred_element_type=jnp.float32
    )
    aggregated = aggregated.reshape(-1, width).astype(jnp.bfloat16)
    pre_act = jnp.dot(seed_features, self_weight, preferred_element_type=jnp.float32)
    pre_act = pre_act + jnp.dot(aggregated, neighbour_weight, preferred_element_type=jnp.float32)
    pre_act = pre_act + layer_bias[None, :]
    sigmoid_val = jax.nn.sigmoid(pre_act)
    slope = sigmoid_val * (1.0 + pre_act * (1.0 - sigmoid_val))
    grad_pre = (cotangent.astype(jnp.float32) * slope).astype(jnp.bfloat16)
    partial_sum = lax.psum_scatter(
        lax.dot_general(
            grad_pre, aggregated, (((0,), (0,)), ((), ())), preferred_element_type=jnp.float32
        ),
        "grp",
        scatter_dimension=0,
        tiled=True,
    )
    return lax.psum_scatter(partial_sum, "rep", scatter_dimension=1, tiled=True)


def solution(mesh):
    placed = (
        P(("grp", "rep"), None),
        P("grp", "rep"),
        P("grp", "rep"),
        P(("grp", "rep"), None),
        P(("grp", "rep"), None),
        P(("grp", "rep"), None, None, None),
        P(),
        P(),
        P(),
        P(("grp", "rep"), None),
    )
    body = fused if (mesh.shape["grp"], mesh.shape["rep"]) == (4, 8) else plain
    return jax.shard_map(
        body, mesh=mesh, in_specs=placed, out_specs=P("grp", "rep"), check_vma=False
    )
```

```python
import functools

import jax
import jax.numpy as jnp
from jax import lax
from jax.experimental import pallas as pl
from jax.experimental.pallas import tpu as pltpu
from jax.sharding import PartitionSpec as P

MESH = pl.DeviceIdType.MESH
BF16 = jnp.bfloat16
F32 = jnp.float32
CHUNKS = ((0, 1), (1, 2), (2, 4))
DIRECT = (0, 1)


def dot(a, b, ca=1, cb=0):
    return lax.dot_general(a, b, (((ca,), (cb,)), ((), ())), preferred_element_type=F32)


def kernel(
    feat_hbm, row_hbm, live_hbm, seed_hbm, block_hbm, tile_hbm, self_hbm, neigh_hbm, bias_hbm, cot_hbm,
    out_ref,
    feat, row, live, seeds, block, tile, w_self, w_neigh, bias, cot,
    request, asked, table_rows, fetched, mixed, hidden, agg_t,
    send_c, recv_c, own, send_1, recv_1, send_2, recv_2, send_3, recv_3, send_m, recv_m,
    load_sem, ask_send, ask_recv, row_send, row_recv,
    c_send, c_recv, s1_send, s1_recv, s2_send, s2_recv, s3_send, s3_recv, m_send, m_recv,
):
    g, r = lax.axis_index("grp"), lax.axis_index("rep")
    x, c = g // 2, g % 2
    z, y = r // 2, r % 2
    n_z = recv_3.shape[0] + 1
    slots = row.shape[1]
    lanes, part = own.shape[-1], own.shape[-2]
    n_f, width_f = fetched.shape[0], fetched.shape[3]
    sib, x_near, x_far = x * 2 + (1 - c), (1 - x) * 2 + c, (1 - x) * 2 + (1 - c)
    group = (x_near, x_far, sib)
    y_near = z * 2 + (1 - y)

    def at(grp, rep):
        return {"grp": grp, "rep": rep}

    loads = {}

    def load(name, src, dst):
        copy = pltpu.make_async_copy(src, dst, load_sem.at[sum(len(v) for v in loads.values())])
        copy.start()
        loads.setdefault(name, []).append(copy)

    def ready(*names):
        for name in names:
            for copy in loads[name]:
                copy.wait()

    hidden_order = (x_far, sib, x_near, g)

    def load_hidden(name, src, dst):
        for k, unit in enumerate(hidden_order):
            cols = pl.ds(pl.multiple_of(unit * lanes, lanes), lanes)
            load(name, src.at[:, cols], dst.at[:, k * lanes : (k + 1) * lanes])

    load("ask", row_hbm, row)
    load("ask", live_hbm, live)

    barrier = pltpu.get_barrier_semaphore()
    for peer in group:
        pl.semaphore_signal(barrier, inc=1, device_id=at(peer, r), device_id_type=MESH)
    pl.semaphore_signal(barrier, inc=1, device_id=at(g, y_near), device_id_type=MESH)
    pl.semaphore_signal(barrier, inc=1, device_id=at(sib, y_near), device_id_type=MESH)
    for d in range(1, n_z):
        pl.semaphore_signal(barrier, inc=1, device_id=at(g, (z + d) % n_z * 2 + y), device_id_type=MESH)
    z_next = z + 1 - 2 * (z % 2)
    pl.semaphore_signal(barrier, inc=1, device_id=at(g, z_next * 2 + 1 - y), device_id_type=MESH)
    pl.semaphore_signal(barrier, inc=1, device_id=at(x_near, z_next * 2 + y), device_id_type=MESH)

    load("feat", feat_hbm, feat)

    ready("ask")
    slot_ix = lax.broadcasted_iota(jnp.int32, (1, slots), 1)
    for p in range(4):
        line = jnp.where(slot_ix < live[0:1, p : p + 1], row[p : p + 1, :], -1)
        line = jnp.broadcast_to(line, (8, slots))
        request[p, :, 0:slots] = line
        request[p, :, slots : 2 * slots] = line
    pl.semaphore_wait(barrier, 6 + n_z)

    asks = []
    for k, peer in enumerate(group):
        copy = pltpu.make_async_remote_copy(
            src_ref=request.at[peer], dst_ref=asked.at[g], send_sem=ask_send.at[k], recv_sem=ask_recv.at[k],
            device_id=at(peer, r), device_id_type=MESH,
        )
        copy.start()
        asks.append(copy)
    asked[g] = request[g]
    load("seeds", seed_hbm, seeds)
    load_hidden("self", self_hbm, w_self)
    load("tile", block_hbm, block)
    load("tile", tile_hbm, tile)
    load_hidden("bias", bias_hbm, bias)
    load_hidden("neigh", neigh_hbm, w_neigh)
    load_hidden("cot", cot_hbm, cot)
    ready("feat")

    def picks(chip):
        lane = lax.broadcasted_iota(jnp.int32, (1, 2 * slots), 1)
        ix = jnp.where(lane < slots, asked[2 * chip][0:1, :], asked[2 * chip + 1][0:1, :])
        column = jnp.broadcast_to(ix, (2 * slots, 2 * slots)).T
        column = jnp.concatenate([column] * (feat.shape[0] // (2 * slots)), axis=1)
        rows_ix = lax.broadcasted_iota(jnp.int32, (2 * slots, feat.shape[0]), 1)
        return jnp.where(rows_ix == column, 1.0, 0.0).astype(BF16)

    def gather(pick, chip, f):
        rows = dot(pick, feat[:, f * width_f : (f + 1) * width_f]).astype(BF16)
        table_rows[f, 2 * chip] = rows[0:slots]
        table_rows[f, 2 * chip + 1] = rows[slots : 2 * slots]

    rows_out = {}

    def send_rows(k, f):
        copy = pltpu.make_async_remote_copy(
            src_ref=table_rows.at[f, group[k]], dst_ref=fetched.at[f, g], send_sem=row_send.at[f, k],
            recv_sem=row_recv.at[f, k], device_id=at(group[k], r), device_id_type=MESH,
        )
        copy.start()
        rows_out[f, k] = copy

    asks[0].wait_recv()
    asks[1].wait_recv()
    pick = picks(1 - x)
    for f in range(n_f):
        gather(pick, 1 - x, f)
        send_rows(0, f)
        send_rows(1, f)
    asks[2].wait_recv()
    pick = picks(x)
    for f in range(n_f):
        gather(pick, x, f)
        send_rows(2, f)
        fetched[f, g] = table_rows[f, g]

    ready("seeds", "self")
    hidden[...] = dot(seeds[...], w_self[...])
    ready("tile")
    n_b, n_k, rows_b, cols_b = tile.shape
    order = block[...]
    for b in range(n_b):
        for j in range(n_k):
            total = jnp.zeros((rows_b, cols_b), F32)
            for k in range(n_k):
                here = jnp.broadcast_to(order[k : k + 1, b : b + 1], (rows_b, cols_b)) == j
                total = jnp.where(here, tile[b, k].astype(F32), total)
            mixed[b * rows_b : (b + 1) * rows_b, j * cols_b : (j + 1) * cols_b] = total.astype(BF16)
    ready("bias", "neigh", "cot")
    hidden[...] += bias[...]

    for f in range(n_f):
        for k in range(3):
            rows_out[f, k].wait_recv()
        cols = slice(f * width_f, (f + 1) * width_f)
        agg = dot(mixed[...], fetched[f].reshape(4 * slots, width_f)).astype(BF16)
        if f < n_f - 1:
            hidden[...] += dot(agg, w_neigh[cols, :])
        agg_t[cols, :] = agg.T

    def grad(side):
        units = slice(side * 2 * lanes, (side + 1) * 2 * lanes)
        pre = hidden[:, units] + dot(agg, w_neigh[cols, units])
        sig = 0.5 * jnp.tanh(0.5 * pre) + 0.5
        return (cot[:, units].astype(F32) * (sig * (1.0 + pre * (1.0 - sig)))).astype(BF16)

    def z_by(m):
        return (z, z + 1 - 2 * (z % 2), (z + 2) % n_z, n_z - 1 - z)[m]

    z_order = tuple(range(n_z - 1, -1, -1))
    bounds = CHUNKS

    def weight_part(grad_side, q, ref, kind):
        lhs = []
        for m in z_order[slice(*bounds[q])]:
            for rep_y in (1 - y, y):
                first = pl.multiple_of((z_by(m) * 2 + rep_y) * 2 * part, 2 * part)
                lhs.append(agg_t[pl.ds(first, 2 * part), :])
        value = dot(jnp.concatenate(lhs, axis=0), grad_side)
        for k in range(bounds[q][1] - bounds[q][0]):
            at_z = bounds[q][0] + k
            for ry in range(2):
                for h in range(2):
                    lo = ((k * 2 + ry) * 2 + h) * part
                    for rx in range(2):
                        piece = value[lo : lo + part, rx * lanes : (rx + 1) * lanes].astype(kind)
                        first, second = (rx, ry) if h == 0 else (ry, rx)
                        if ref is own and q in DIRECT and first == 0:
                            send_1[h, second, at_z] = piece.astype(BF16)
                        else:
                            ref[h, first, second, at_z] = piece

    def exchange(src, dst, sends, recvs, peer):
        copy = pltpu.make_async_remote_copy(
            src_ref=src, dst_ref=dst, send_sem=sends, recv_sem=recvs, device_id=peer, device_id_type=MESH
        )
        copy.start()
        return copy

    near = (at(x_near, r), at(g, y_near))
    far = (at(x_far, r), at(sib, y_near))
    core_out, outs_1, outs_2, outs_3, outs_m = {}, {}, {}, [], []
    cross = (at(g, z_by(1) * 2 + 1 - y), at(x_near, z_by(1) * 2 + y))

    def to_core(q, k, peer, *part_of):
        place = part_of + (pl.ds(bounds[q][0], bounds[q][1] - bounds[q][0]),)
        k = q * 3 + k
        return exchange(send_c.at[place], recv_c.at[place], c_send.at[k], c_recv.at[k], peer)

    every = slice(None)
    chunks = range(len(bounds))
    grad_side = grad(0)
    for q in chunks:
        weight_part(grad_side, q, send_c, BF16)
        if q in DIRECT:
            core_out[q] = [to_core(q, h, far[h], h, 0, every) for h in range(2)]
            core_out[q].append(to_core(q, 2, at(sib, r), every, 1, every))
        else:
            core_out[q] = [to_core(q, 0, at(sib, r), every, every, every)]
    grad_side = grad(1)
    for q in chunks:
        weight_part(grad_side, q, own, F32)
        zs = slice(*bounds[q])
        sl = pl.ds(bounds[q][0], bounds[q][1] - bounds[q][0])
        if q not in DIRECT:
            core_out[q][0].wait_recv()
        for h in range(2):
            if q not in DIRECT:
                send_1[h, :, zs] = (own[h, 0, :, zs] + recv_c[h, 0, :, zs].astype(F32)).astype(BF16)
            k = q * 2 + h
            outs_1[q, h] = exchange(send_1.at[h, :, sl], recv_1.at[h, :, sl], s1_send.at[k], s1_recv.at[k], near[h])
    def after_first(q, h):
        zs = slice(*bounds[q])
        kept = own[h, 1, :, zs] + recv_c[h, 1, :, zs].astype(F32)
        if q in DIRECT:
            core_out[q][h].wait_recv()
            kept = kept + recv_c[h, 0, :, zs].astype(F32)
        outs_1[q, h].wait_recv()
        return kept + recv_1[h, :, zs].astype(F32)

    def second(q):
        zs = slice(*bounds[q])
        sl = pl.ds(bounds[q][0], bounds[q][1] - bounds[q][0])
        core_out[q][2].wait_recv()
        for h in range(2):
            kept = after_first(q, h)
            send_2[h, zs] = kept[0].astype(BF16)
            k = q * 2 + h
            outs_2[q, h] = exchange(send_2.at[h, sl], recv_2.at[h, sl], s2_send.at[k], s2_recv.at[k], near[1 - h])
            own[h, 1, 1, zs] = kept[1]

    def third(q):
        for h in range(2):
            outs_2[q, h].wait_recv()
            for at_z in range(*bounds[q]):
                done = own[h, 1, 1, at_z] + recv_2[h, at_z].astype(F32)
                send_3[z_order[at_z] - 1, h] = done.astype(BF16)
        for m in z_order[slice(*bounds[q])]:
            to = at(g, z_by(m) * 2 + y)
            outs_3.append(exchange(send_3.at[m - 1], recv_3.at[m - 1], s3_send.at[m - 1], s3_recv.at[m - 1], to))

    def second_and_third(q):
        for h in range(2):
            kept = after_first(q, h)
            send_m[h, 0] = kept[0, 0].astype(BF16)
            send_m[h, 1] = kept[1, 0].astype(BF16)
            send_m[h, 2] = kept[0, 1].astype(BF16)
            peers = (cross[h], at(g, z_by(1) * 2 + y), near[1 - h])
            for i in range(3):
                k = h * 3 + i
                outs_m.append(exchange(send_m.at[h, i], recv_m.at[h, i], m_send.at[k], m_recv.at[k], peers[i]))
            own[h, 1, 1, n_z - 1] = kept[1, 1]

    second(0)
    second(1)
    third(0)
    second_and_third(2)
    third(1)
    for copies in (asks, rows_out.values(), *core_out.values(), outs_1.values(), outs_2.values(), outs_3, outs_m):
        for copy in copies:
            copy.wait_send()
    total = jnp.concatenate([own[h, 1, 1, n_z - 1] for h in range(2)], axis=0)
    for copy in outs_m:
        copy.wait_recv()
    for i in range(3):
        total = total + jnp.concatenate([recv_m[h, i].astype(F32) for h in range(2)], axis=0)
    for copy in outs_3:
        copy.wait_recv()
    for d in range(1, n_z - 1):
        total = total + recv_3[d].astype(F32).reshape(total.shape)
    out_ref[...] = total


def fused(features, fetch_row, live_count, seed_features, tile_block, tile_weight, self_weight, neighbour_weight, layer_bias, cotangent):
    width, hid = neighbour_weight.shape
    seeds = seed_features.shape[0]
    slots = fetch_row.shape[1]
    n_z, n_f = 4, 6
    lanes = hid // 4
    part = width // (4 * n_z)
    bias = layer_bias.reshape(1, hid)
    operands = (features, fetch_row, live_count.T, seed_features, tile_block.T, tile_weight, self_weight, neighbour_weight, bias, cotangent)
    n_b, n_k, rows_b, cols_b = tile_weight.shape
    vmem = pltpu.VMEM
    dma = pltpu.SemaphoreType.DMA
    result = pl.pallas_call(
        kernel,
        out_shape=vmem((width // (2 * n_z), lanes), F32),
        in_specs=[pl.BlockSpec(memory_space=pltpu.HBM)] * len(operands),
        out_specs=pl.BlockSpec(memory_space=vmem),
        scratch_shapes=[vmem(a.shape, a.dtype) for a in operands] + [
            vmem((4, 8, 2 * slots), jnp.int32),
            vmem((4, 8, 2 * slots), jnp.int32),
            vmem((n_f, 4, slots, width // n_f), BF16),
            vmem((n_f, 4, slots, width // n_f), BF16),
            vmem((seeds, n_k * cols_b), BF16),
            vmem((seeds, hid), F32),
            vmem((width, seeds), BF16),
            vmem((2, 2, 2, n_z, part, lanes), BF16),
            vmem((2, 2, 2, n_z, part, lanes), BF16),
            vmem((2, 2, 2, n_z, part, lanes), F32),
            vmem((2, 2, n_z, part, lanes), BF16),
            vmem((2, 2, n_z, part, lanes), BF16),
            vmem((2, n_z, part, lanes), BF16),
            vmem((2, n_z, part, lanes), BF16),
            vmem((n_z - 1, 2, part, lanes), BF16),
            vmem((n_z - 1, 2, part, lanes), BF16),
            vmem((2, 3, part, lanes), BF16),
            vmem((2, 3, part, lanes), BF16),
            dma((22,)), dma((3,)), dma((3,)), dma((n_f, 3)), dma((n_f, 3)),
            *[dma((3 * len(CHUNKS),))] * 2, *[dma((2 * len(CHUNKS),))] * 4, dma((n_z - 1,)), dma((n_z - 1,)), dma((6,)), dma((6,)),
        ],
        compiler_params=pltpu.CompilerParams(
            collective_id=0, has_side_effects=True, vmem_limit_bytes=56 * 1024 * 1024
        ),
        name="sage_step",
    )(*operands)
    return result.T


def plain(
    features,
    fetch_row,
    live_count,
    seed_features,
    tile_block,
    tile_weight,
    self_weight,
    neighbour_weight,
    layer_bias,
    cotangent,
):
    width = features.shape[1]
    asked = lax.all_to_all(fetch_row, "grp", split_axis=0, concat_axis=0, tiled=True)
    table_rows = jnp.take(features, asked.reshape(-1), axis=0).reshape(asked.shape + (width,))
    fetched = lax.all_to_all(table_rows, "grp", split_axis=0, concat_axis=0, tiled=True)
    live_mask = lax.broadcasted_iota(jnp.int32, fetch_row.shape, 1) < live_count
    fetched = jnp.where(live_mask[:, :, None], fetched, jnp.zeros((), fetched.dtype))
    row_blocks = fetched.reshape(-1, 128, width)
    chosen = jnp.take(row_blocks, tile_block, axis=0)
    aggregated = jnp.einsum(
        "bkij,bkjf->bif", tile_weight, chosen, preferred_element_type=jnp.float32
    )
    aggregated = aggregated.reshape(-1, width).astype(jnp.bfloat16)
    pre_act = jnp.dot(seed_features, self_weight, preferred_element_type=jnp.float32)
    pre_act = pre_act + jnp.dot(aggregated, neighbour_weight, preferred_element_type=jnp.float32)
    pre_act = pre_act + layer_bias[None, :]
    sigmoid_val = jax.nn.sigmoid(pre_act)
    slope = sigmoid_val * (1.0 + pre_act * (1.0 - sigmoid_val))
    grad_pre = (cotangent.astype(jnp.float32) * slope).astype(jnp.bfloat16)
    partial_sum = lax.psum_scatter(
        lax.dot_general(
            grad_pre, aggregated, (((0,), (0,)), ((), ())), preferred_element_type=jnp.float32
        ),
        "grp",
        scatter_dimension=0,
        tiled=True,
    )
    return lax.psum_scatter(partial_sum, "rep", scatter_dimension=1, tiled=True)


def solution(mesh):
    placed = (
        P(("grp", "rep"), None),
        P("grp", "rep"),
        P("grp", "rep"),
        P(("grp", "rep"), None),
        P(("grp", "rep"), None),
        P(("grp", "rep"), None, None, None),
        P(),
        P(),
        P(),
        P(("grp", "rep"), None),
    )
    body = fused if (mesh.shape["grp"], mesh.shape["rep"]) == (4, 8) else plain
    return jax.shard_map(
        body, mesh=mesh, in_specs=placed, out_specs=P("grp", "rep"), check_vma=False
    )
```
